128 devices in a mesh: dp: 4 (over z), mem: 32 (over x, y, core).
Axes of the slice: x: 4, y: 4, z: 4, core: 2. Of those that a mesh axis runs over, the one named last changes fastest.
Arguments:
- queries: bfloat16 [8192, 2048], P('dp'), may hold values from -9 to 9
- grad_out: bfloat16 [8192, 2048], P('dp'), may hold values from -192 to 192
- mem_keys: bfloat16 [16384, 2048], P('mem'), may hold values from -4 to 4
- mem_values: bfloat16 [16384, 2048], P('mem'), may hold values from -6 to 6
- block_lists: int32 [64, 16], P('dp'), may hold values from 0 to 127, all different within a row
- block_home: int32 [128], replicated, may hold values from 0 to 127, each once
Outputs:
- grad_queries: bfloat16 [8192, 2048], P(('dp', 'mem'))
- grad_keys: bfloat16 [16384, 2048], P('mem')
- grad_values: bfloat16 [16384, 2048], P('mem')
The draws below stay inside these ranges and needn't reach their ends.
Inputs may be any that keep to these rules, and one draw needn't show every extreme that they name: `block_lists`: each row names 16 different memory blocks; every block is named by some row, some blocks far more often than others. `block_home`: each stored block holds exactly one memory block; stored block j lies on index j // 4 of mem.
All inputs are finite; a program needn't handle non-finite values.
Results may differ from the reference program's by a relative error of at most 0.0085.
Values may be sent and summed in bfloat16 or wider, within the bound.
No kernel may reach another device: no remote copies, remote signals or barrier semaphores. Data moves between devices by JAX's collectives and lax.ppermute only.
A program may use at most 192 MiB of HBM per device.

```python
import jax
import jax.numpy as jnp
from jax import lax

H = 16
DH = 128
BLK = 128
TOPB = 16
HD = 2048
QBLKS = 64
QTOK = 8192
NBLK = 128
MROWS = 16384


def draw_queries(key, part):
    key = jax.random.fold_in(key, 11)
    first = jax.random.fold_in(key, 0)
    base = jnp.clip(jax.random.normal(first, (QTOK, H * DH), jnp.float32), -4.0, 4.0)
    return base.astype(jnp.bfloat16)


def draw_mem_keys(key, part):
    key = jax.random.fold_in(key, 23)
    base = jnp.clip(jax.random.normal(key, (MROWS, H * DH), jnp.float32), -4.0, 4.0)
    return base.astype(jnp.bfloat16)


def level_of(own_key, shape, shards, smallest, high):
    level, own = 1.0, jax.random.fold_in(own_key, 6)
    for axis_at, blocks in shards:
        heights = jnp.exp(jax.random.uniform(jax.random.fold_in(own, axis_at), (blocks,), jnp.float32, smallest / len(shards), high / len(shards)))
        level = level * jnp.repeat(heights, shape[axis_at] // blocks).reshape([-1 if axis == axis_at else 1 for axis in range(len(shape))])
    return level


def different_ones(rng, rows, number_of, top, lift):
    ranking = jax.random.permutation(jax.random.fold_in(rng, 1), number_of)
    favour = ranking
    for power in range(3):
        favour = favour * favour // number_of
    favour = favour * lift // number_of
    tickets = jax.random.randint(jax.random.fold_in(rng, 2), (rows, number_of), 0, 4096) + favour
    holders = jax.random.permutation(jax.random.fold_in(rng, 3), rows)[jnp.arange(number_of) % rows]
    tickets = jnp.where(jnp.arange(rows)[:, None] == holders[None, :], 1 << 14, tickets)
    merit = tickets * number_of + jnp.arange(number_of)
    return lax.top_k(merit.astype(jnp.int32), top)[1].astype(jnp.int32)


def scatter_about(rng, dims, deviation, most, pieces=(), kind=jnp.bfloat16):
    entries = jax.random.normal(rng, dims, jnp.float32) * deviation
    if len(pieces) > 0:
        entries = level_of(rng, dims, pieces, -0.22, 0.18) * entries
    return jnp.clip(entries, min=-most, max=most).astype(kind)


def setup_inputs(seed: int = 0) -> dict:
    seeds = jax.random.split(jax.random.key(seed), 7)
    queries = draw_queries(jax.random.fold_in(seeds[6], 71), 0)
    grad_out = scatter_about(seeds[1], (QTOK, HD), 32.0, 192.0, ((0, 4),))
    mem_keys = draw_mem_keys(jax.random.fold_in(seeds[6], 71), 0)
    mem_values = scatter_about(seeds[3], (MROWS, HD), 1.0, 6.0, ((0, 32),))
    block_lists = different_ones(seeds[4], QBLKS, NBLK, TOPB, 2048)
    block_home = jax.random.permutation(seeds[5], NBLK).astype(jnp.int32)
    return dict(queries=queries, grad_out=grad_out, mem_keys=mem_keys, mem_values=mem_values, block_lists=block_lists, block_home=block_home)


def round_keep(values):
    return lax.optimization_barrier(values.astype(jnp.bfloat16)).astype(jnp.float32)


def reference(queries, grad_out, mem_keys, mem_values, block_lists, block_home):
    scale = DH ** -0.5
    slots = block_home[block_lists]
    offsets = jnp.arange(BLK, dtype=jnp.int32)

    def one_block(carry, index):
        grad_k, grad_v = carry
        start = (index * BLK).astype(jnp.int32)
        qrow = lax.dynamic_slice_in_dim(queries, start, BLK, 0).astype(jnp.float32).reshape(BLK, H, DH)
        drow = lax.dynamic_slice_in_dim(grad_out, start, BLK, 0).astype(jnp.float32).reshape(BLK, H, DH)
        rows = (slots[index][:, None] * BLK + offsets[None, :]).reshape(-1).astype(jnp.int32)
        keys = jnp.take(mem_keys, rows, axis=0).astype(jnp.float32).reshape(TOPB, BLK, H, DH)
        values = jnp.take(mem_values, rows, axis=0).astype(jnp.float32).reshape(TOPB, BLK, H, DH)
        scores = jnp.einsum('qhd,tkhd->thqk', qrow, keys) * scale
        highs = jnp.max(scores, axis=-1)
        expo = jnp.exp(scores - highs[..., None])
        totals = jnp.sum(expo, axis=-1)
        partial_out = jnp.einsum('thqk,tkhd->tqhd', round_keep(expo), values)
        products = jnp.swapaxes(jnp.sum(drow[None] * partial_out, axis=-1), 1, 2)
        top = jnp.max(highs, axis=0)
        weights = jnp.exp(highs - top[None])
        total_sum = jnp.sum(weights * totals, axis=0)
        total_prod = jnp.sum(weights * products, axis=0)
        lse = top + jnp.log(total_sum)
        delta = total_prod / total_sum
        probs = jnp.exp(scores - lse[None, :, :, None])
        grad_vb = jnp.einsum('thqk,qhd->tkhd', round_keep(probs), drow)
        dprob = jnp.einsum('qhd,tkhd->thqk', drow, values)
        dscore = round_keep(probs * (dprob - delta[None, :, :, None]) * scale)
        grad_q = jnp.einsum('thqk,tkhd->qhd', dscore, keys)
        grad_kb = jnp.einsum('thqk,qhd->tkhd', dscore, qrow)
        grad_k = grad_k.at[rows].add(grad_kb.reshape(TOPB * BLK, H * DH))
        grad_v = grad_v.at[rows].add(grad_vb.reshape(TOPB * BLK, H * DH))
        return (grad_k, grad_v), grad_q.reshape(BLK, H * DH).astype(jnp.bfloat16)

    zeros = jnp.zeros((MROWS, H * DH), jnp.float32)
    (grad_k, grad_v), grad_q = lax.scan(one_block, (zeros, zeros), jnp.arange(QBLKS, dtype=jnp.int32))
    return grad_q.reshape(QTOK, H * DH), grad_k.astype(jnp.bfloat16), grad_v.astype(jnp.bfloat16)
```

```python
import jax
import jax.numpy as jnp
from jax import lax
from jax.experimental import pallas as pl
from jax.experimental.pallas import tpu as pltpu
from jax.sharding import PartitionSpec as P

H = 16
DH = 128
BLK = 128
TOPB = 16
NZ = 4
NCHIP = 16
QPER = 8
NQ = NZ * QPER
NB = 2 * NCHIP
NENT = NQ * TOPB
UNROLL_F = 8
UNROLL_B = 4
SCALE = DH ** (-0.5)
BF = jnp.bfloat16
F32 = jnp.float32
MB = 1 << 20


NT = (((1,), (1,)), ((), ()))
NN = (((1,), (0,)), ((), ()))
TN = (((0,), (0,)), ((), ()))


def dot(a, b, dims):
    return lax.dot_general(a, b, dims, preferred_element_type=F32)


def over_z(array, shift):
    return lax.ppermute(array, "dp", [(i, (i + shift) % NZ) for i in range(NZ)])


def swap_cores(array):
    return lax.ppermute(array, "mem", [(i, i ^ 1) for i in range(2 * NCHIP)])


def plane_exchange(array):
    groups = [[2 * c + k for c in range(NCHIP)] for k in range(2)]
    return lax.all_to_all(array, "mem", 0, 0, axis_index_groups=groups)


def list_kernel(place, l0, l1, l2, l3, home, ents, count):
    z = place[0]
    k = place[1]

    def group(r, lists, n):
        def block(i, n):
            q = r * QPER + i
            seen = jnp.int32(0)
            for t in range(TOPB):
                slot = home[lists[i, t]]
                mine = (slot & 3) == z
                owner = slot >> 2
                b = ((owner & 1) ^ k) * NCHIP + (owner >> 1)
                ents[n] = (q << 15) | ((seen * NQ + q) << 5) | b
                step = mine.astype(jnp.int32)
                n = n + step
                seen = seen + step
            return n

        return lax.fori_loop(0, QPER, block, n)

    n = jnp.int32(0)
    for r, lists in enumerate((l0, l1, l2, l3)):
        n = group(r, lists, n)
    for u in range(8):
        ents[n + u] = (NQ << 15) | (NENT << 5)
    count[0] = n


def make_list(place, lists, home):
    smem = pl.BlockSpec(memory_space=pltpu.SMEM)
    return pl.pallas_call(
        list_kernel,
        out_shape=(
            jax.ShapeDtypeStruct((NENT + 8,), jnp.int32),
            jax.ShapeDtypeStruct((8,), jnp.int32),
        ),
        in_specs=[smem] * 6,
        out_specs=(smem, smem),
        name="entry_list",
    )(place, *lists, home)


def fetch(qrefs, grefs, kvrefs, qs, gs, kv, sems):
    copies = []
    for r in range(NZ):
        copies.append(pltpu.make_async_copy(qrefs[r], qs.at[r], sems.at[r]))
        copies.append(pltpu.make_async_copy(grefs[r], gs.at[r], sems.at[NZ + r]))
    for p in range(4):
        to = kv.at[p % 2, p // 2]
        copies.append(pltpu.make_async_copy(kvrefs[p], to, sems.at[2 * NZ + p]))
    for copy in copies:
        copy.start()
    return copies


def unpack(p):
    q = p >> 15
    b = p & 31
    return (q >> 3) & 3, q & 7, q, (p >> 5) & 1023, b >> 4, b & 15


def fwd_kernel(ents, count, q0, q1, q2, q3, g0, g1, g2, g3, ka, va, kb, vb, out, qs, gs, kv, st, sems):
    copies = fetch((q0, q1, q2, q3), (g0, g1, g2, g3), (ka, va, kb, vb), qs, gs, kv, sems)
    st[0] = jnp.full((NENT + 8, DH), -1e30, F32)
    st[1] = jnp.zeros((NENT + 8, DH), F32)
    st[2] = jnp.zeros((NENT + 8, DH), F32)
    for copy in copies:
        copy.wait()

    def body(n, carry):
        parts = [unpack(ents[UNROLL_F * n + u]) for u in range(UNROLL_F)]
        scores = [dot(kv[0, p[4], p[5]], qs[p[0], p[1]], NT) * SCALE for p in parts]
        dprob = [dot(kv[1, p[4], p[5]], gs[p[0], p[1]], NT) for p in parts]
        highs = [jnp.max(x, axis=0, keepdims=True) for x in scores]
        expo = [jnp.exp(x - high) for x, high in zip(scores, highs)]
        for p, high, e, d in zip(parts, highs, expo, dprob):
            row = pl.ds(p[3], 1)
            st[0, row, :] = high
            st[1, row, :] = jnp.sum(e, axis=0, keepdims=True)
            st[2, row, :] = jnp.sum(e.astype(BF).astype(F32) * d, axis=0, keepdims=True)
        return carry

    lax.fori_loop(0, (count[0] + UNROLL_F - 1) // UNROLL_F, body, 0)
    high = st[0, 0:NQ]
    for e in range(1, TOPB):
        high = jnp.maximum(high, st[0, e * NQ : (e + 1) * NQ])
    total = jnp.zeros((NQ, DH), F32)
    prod = jnp.zeros((NQ, DH), F32)
    for e in range(TOPB):
        rows = slice(e * NQ, (e + 1) * NQ)
        weight = jnp.exp(st[0, rows] - high)
        total = total + weight * st[1, rows]
        prod = prod + weight * st[2, rows]
    out[0] = high
    out[1] = total
    out[2] = prod


def scratch_in():
    return [
        pltpu.VMEM((NZ, QPER, BLK, DH), BF),
        pltpu.VMEM((NZ, QPER, BLK, DH), BF),
        pltpu.VMEM((2, 2, NCHIP, BLK, DH), BF),
    ]


def forward(ents, count, qparts, gparts, kvs):
    smem = pl.BlockSpec(memory_space=pltpu.SMEM)
    far = pl.BlockSpec(memory_space=pl.ANY)
    return pl.pallas_call(
        fwd_kernel,
        out_shape=jax.ShapeDtypeStruct((3, NQ, DH), F32),
        in_specs=[smem, smem] + [far] * 12,
        out_specs=pl.BlockSpec(memory_space=pltpu.VMEM),
        scratch_shapes=scratch_in()
        + [pltpu.VMEM((3, NENT + 8, DH), F32), pltpu.SemaphoreType.DMA((2 * NZ + 4,))],
        compiler_params=pltpu.CompilerParams(vmem_limit_bytes=24 * MB),
        name="forward",
    )(ents, count, *qparts, *gparts, *kvs)


def bwd_kernel(
    ents, count, s0, s1, s2, s3, q0, q1, q2, q3, g0, g1, g2, g3, ka, va, kb, vb,
    dq0, dq1, dq2, dq3, kown, vown, kother, vother,
    qs, gs, kv, dq, dk, dv, lse, delta, sems,
):
    copies = fetch((q0, q1, q2, q3), (g0, g1, g2, g3), (ka, va, kb, vb), qs, gs, kv, sems)

    def clear(i, carry):
        zero = jnp.zeros((BLK, DH), F32)
        dq[i] = zero
        dk[i] = zero
        dv[i] = zero
        return carry

    lax.fori_loop(0, NQ, clear, 0)
    for r in range(NZ):
        rows = slice(r * QPER, (r + 1) * QPER)
        parts = []
        for ref, shift in ((s0, 0), (s1, 1), (s2, 2), (s3, 3)):
            at = (r + shift) % NZ
            parts.append([ref[n, at * QPER : (at + 1) * QPER] for n in range(3)])
        high = jnp.maximum(
            jnp.maximum(parts[0][0], parts[1][0]), jnp.maximum(parts[2][0], parts[3][0])
        )
        total = jnp.zeros((QPER, DH), F32)
        prod = jnp.zeros((QPER, DH), F32)
        for part in parts:
            weight = jnp.exp(part[0] - high)
            total = total + weight * part[1]
            prod = prod + weight * part[2]
        lse[rows] = high + jnp.log(total)
        delta[rows] = prod / total
    for copy in copies:
        copy.wait()

    lse[NQ : NQ + 8] = jnp.full((8, DH), 1e30, F32)
    delta[NQ : NQ + 8] = jnp.zeros((8, DH), F32)

    def body(n, carry):
        parts = [unpack(ents[UNROLL_B * n + u]) for u in range(UNROLL_B)]
        keys = [kv[0, p[4], p[5]] for p in parts]
        quer = [qs[p[0], p[1]] for p in parts]
        grad = [gs[p[0], p[1]] for p in parts]
        scores = [dot(a, b, NT) * SCALE for a, b in zip(keys, quer)]
        dprob = [dot(kv[1, p[4], p[5]], b, NT) for p, b in zip(parts, grad)]
        probs = [jnp.exp(x - lse[pl.ds(p[2], 1), :]) for x, p in zip(scores, parts)]
        dscore = [
            (x * (d - delta[pl.ds(p[2], 1), :]) * SCALE).astype(BF)
            for x, d, p in zip(probs, dprob, parts)
        ]
        gv = [dot(x.astype(BF), b, NN) for x, b in zip(probs, grad)]
        gk = [dot(x, b, NN) for x, b in zip(dscore, quer)]
        gq = [dot(x, b, TN) for x, b in zip(dscore, keys)]
        for p, a, b, c in zip(parts, gv, gk, gq):
            at = p[4] * NCHIP + p[5]
            dv[at] += a
            dk[at] += b
            dq[p[0] * QPER + p[1]] += c
        return carry

    lax.fori_loop(0, (count[0] + UNROLL_B - 1) // UNROLL_B, body, 0)
    for r, ref in enumerate((dq0, dq1, dq2, dq3)):
        ref[...] = dq[r * QPER : (r + 1) * QPER].astype(ref.dtype)
    kown[...] = dk[:NCHIP]
    vown[...] = dv[:NCHIP]
    kother[...] = dk[NCHIP:].astype(BF)
    vother[...] = dv[NCHIP:].astype(BF)


def backward(ents, count, stats, qparts, gparts, kvs):
    smem = pl.BlockSpec(memory_space=pltpu.SMEM)
    vmem = pl.BlockSpec(memory_space=pltpu.VMEM)
    far = pl.BlockSpec(memory_space=pl.ANY)
    tile = (BLK, DH)
    outs = [jax.ShapeDtypeStruct((QPER,) + tile, F32)]
    outs += [jax.ShapeDtypeStruct((QPER,) + tile, BF)] * 3
    outs += [jax.ShapeDtypeStruct((NCHIP,) + tile, F32)] * 2
    outs += [jax.ShapeDtypeStruct((NCHIP,) + tile, BF)] * 2
    return pl.pallas_call(
        bwd_kernel,
        out_shape=tuple(outs),
        in_specs=[smem, smem] + [vmem] * 4 + [far] * 12,
        out_specs=tuple([vmem] * 8),
        scratch_shapes=scratch_in()
        + [
            pltpu.VMEM((NQ,) + tile, F32),
            pltpu.VMEM((NB,) + tile, F32),
            pltpu.VMEM((NB,) + tile, F32),
            pltpu.VMEM((NQ + 8, DH), F32),
            pltpu.VMEM((NQ + 8, DH), F32),
            pltpu.SemaphoreType.DMA((2 * NZ + 4,)),
        ],
        compiler_params=pltpu.CompilerParams(vmem_limit_bytes=40 * MB),
        name="backward",
    )(ents, count, *stats, *qparts, *gparts, *kvs)


def place_kernel(place, k0, k1, k2, k3, v0, v1, v2, v3, outk, outv, sems):
    z = place[0]
    copies = []
    for r, (kr, vr) in enumerate(((k0, v0), (k1, v1), (k2, v2), (k3, v3))):
        rows = pl.ds(pl.multiple_of(((z + r) & 3) * BLK, BLK), BLK)
        copies.append(pltpu.make_async_copy(kr, outk.at[rows], sems.at[2 * r]))
        copies.append(pltpu.make_async_copy(vr, outv.at[rows], sems.at[2 * r + 1]))
    for copy in copies:
        copy.start()
    for copy in copies:
        copy.wait()


def place_blocks(place, kparts, vparts):
    smem = pl.BlockSpec(memory_space=pltpu.SMEM)
    far = pl.BlockSpec(memory_space=pl.ANY)
    shape = jax.ShapeDtypeStruct((NZ * BLK, H * DH), BF)
    return pl.pallas_call(
        place_kernel,
        out_shape=(shape, shape),
        in_specs=[smem] + [pl.BlockSpec(memory_space=pltpu.VMEM)] * 8,
        out_specs=(far, far),
        scratch_shapes=[pltpu.SemaphoreType.DMA((2 * NZ,))],
        compiler_params=pltpu.CompilerParams(vmem_limit_bytes=16 * MB),
        name="place_blocks",
    )(place, *kparts, *vparts)


def heads_first(array):
    return jnp.transpose(array.reshape(array.shape[0], H, DH), (1, 0, 2))


def rows_first(array):
    return jnp.transpose(array, (1, 0, 2)).reshape(array.shape[1], H * DH)


def per_device(queries, grad_out, mem_keys, mem_values, block_lists, block_home):
    z = lax.axis_index("dp")
    m = lax.axis_index("mem")
    c, k = m // 2, m % 2
    place = jnp.stack([z, k]).astype(jnp.int32)

    kz = heads_first(lax.dynamic_slice_in_dim(mem_keys, z * BLK, BLK, 0))
    vz = heads_first(lax.dynamic_slice_in_dim(mem_values, z * BLK, BLK, 0))
    k_got, v_got = plane_exchange(kz), plane_exchange(vz)

    rows = QPER * BLK
    mine = (k * rows, c * DH)
    tiles = (QPER, BLK, DH)
    q_own = lax.dynamic_slice(queries, mine, (rows, DH)).reshape(tiles)
    g_own = lax.dynamic_slice(grad_out, mine, (rows, DH)).reshape(tiles)
    l_own = lax.dynamic_slice_in_dim(block_lists, k * QPER, QPER, 0)
    q_prev = over_z(q_own, 1)
    g_next = over_z(g_own, -1)
    g_prev = over_z(g_own, 1)
    q_next = over_z(q_own, -1)
    q_far = over_z(q_prev, 1)
    g_far = over_z(g_next, -1)
    lists = (l_own, over_z(l_own, -1), over_z(l_own, 2), over_z(l_own, 1))
    ents, count = make_list(place, lists, block_home)
    qparts = (q_own, q_next, q_far, q_prev)
    gparts = (g_own, g_next, g_far, g_prev)
    kvs = (k_got, v_got, swap_cores(k_got), swap_cores(v_got))

    stat = forward(ents, count, qparts, gparts, kvs)
    stats = (stat, over_z(stat, 1), over_z(stat, 2), over_z(stat, -1))
    dq0, dq1, dq2, dq3, kown, vown, kother, vother = backward(
        ents, count, stats, qparts, gparts, kvs
    )

    v_sum = (vown + swap_cores(vother).astype(F32)).astype(BF)
    k_sum = (kown + swap_cores(kother).astype(F32)).astype(BF)
    v_own = rows_first(plane_exchange(v_sum))
    k_own = rows_first(plane_exchange(k_sum))
    v_prev = over_z(v_own, 1)
    v_next = over_z(v_own, -1)
    k_prev = over_z(k_own, 1)
    k_next = over_z(k_own, -1)
    v_far = over_z(v_prev, 1)
    k_far = over_z(k_next, -1)
    grad_keys, grad_values = place_blocks(
        place, (k_own, k_next, k_far, k_prev), (v_own, v_next, v_far, v_prev)
    )

    dq_sum = (
        dq0
        + over_z(dq1, 1).astype(F32)
        + over_z(dq3, -1).astype(F32)
        + over_z(dq2, 2).astype(F32)
    ).astype(BF)
    half = BLK // 2
    keep = lax.dynamic_slice_in_dim(dq_sum, k * half, half, 1)
    give = lax.dynamic_slice_in_dim(dq_sum, (1 - k) * half, half, 1)
    got = swap_cores(give)
    whole = jnp.where(
        k == 0, jnp.concatenate([keep, got], axis=0), jnp.concatenate([got, keep], axis=0)
    )
    grad_queries = rows_first(plane_exchange(whole))
    return grad_queries, grad_keys, grad_values


def solution(mesh):
    in_specs = (P("dp", None), P("dp", None), P("mem", None), P("mem", None), P("dp", None), P())
    out_specs = (P(("dp", "mem"), None), P("mem", None), P("mem", None))
    return jax.shard_map(
        per_device, mesh=mesh, in_specs=in_specs, out_specs=out_specs, check_vma=False
    )
```

```python
import jax
import jax.numpy as jnp
from jax import lax
from jax.experimental import pallas as pl
from jax.experimental.pallas import tpu as pltpu
from jax.sharding import PartitionSpec as P

H = 16
DH = 128
BLK = 128
TOPB = 16
NZ = 4
NCHIP = 16
QPER = 8
NQ = NZ * QPER
NB = 2 * NCHIP
NENT = NQ * TOPB
COUNT = NENT + 8
NCOPY = 2 * NZ + 2
UNROLL_F = 8
UNROLL_B = 8
SCALE = DH ** (-0.5)
BF = jnp.bfloat16
F32 = jnp.float32
MB = 1 << 20


NT = (((1,), (1,)), ((), ()))
NN = (((1,), (0,)), ((), ()))
TN = (((0,), (0,)), ((), ()))


def dot(a, b, dims):
    return lax.dot_general(a, b, dims, preferred_element_type=F32)


def over_z(array, shift):
    return lax.ppermute(array, "dp", [(i, (i + shift) % NZ) for i in range(NZ)])


def swap_cores(array):
    return lax.ppermute(array, "mem", [(i, i ^ 1) for i in range(2 * NCHIP)])


def plane_exchange(array):
    groups = [[2 * c + k for c in range(NCHIP)] for k in range(2)]
    return lax.all_to_all(array, "mem", 0, 0, axis_index_groups=groups)


def prepare_kernel(place, lists, queries, grads, keys, values, q, g, kv, sems):
    z, c, k = place[0], place[1], place[2]
    cols = pl.ds(pl.multiple_of(c * DH, DH), DH)
    pairs = []
    for i in range(QPER):
        rows = pl.ds(pl.multiple_of((k * QPER + i) * BLK, BLK), BLK)
        pairs.append((queries.at[rows, cols], q.at[i]))
        pairs.append((grads.at[rows, cols], g.at[i]))
    rows = pl.ds(pl.multiple_of(z * BLK, BLK), BLK)
    for h in range(H):
        cols = slice(h * DH, (h + 1) * DH)
        pairs.append((keys.at[rows, cols], kv.at[h, :BLK]))
        pairs.append((values.at[rows, cols], kv.at[h, BLK:]))
    copies = [pltpu.make_async_copy(a, b, sems.at[n]) for n, (a, b) in enumerate(pairs)]
    for copy in copies:
        copy.start()
    q[QPER, :TOPB, :TOPB] = lists[...].astype(F32).astype(BF)
    for copy in copies:
        copy.wait()


def prepare(place, queries, grads, keys, values, lists):
    smem = pl.BlockSpec(memory_space=pltpu.SMEM)
    vmem = pl.BlockSpec(memory_space=pltpu.VMEM)
    hbm = pl.BlockSpec(memory_space=pltpu.HBM)
    return pl.pallas_call(
        prepare_kernel,
        out_shape=(
            jax.ShapeDtypeStruct((QPER + 1, BLK, DH), BF),
            jax.ShapeDtypeStruct((QPER, BLK, DH), BF),
            jax.ShapeDtypeStruct((H, 2 * BLK, DH), BF),
        ),
        in_specs=[smem, vmem] + [hbm] * 4,
        out_specs=(vmem, vmem, vmem),
        scratch_shapes=[pltpu.SemaphoreType.DMA((2 * QPER + 2 * H,))],
        compiler_params=pltpu.CompilerParams(vmem_limit_bytes=60 * MB),
        name="prepare",
    )(place, lists, queries, grads, keys, values)


def list_kernel(place, l0, l1, l2, l3, home, ents):
    z = place[0]
    k = place[2]

    def group(r, lists, n):
        def block(i, n):
            q = r * QPER + i
            seen = jnp.int32(0)
            for t in range(TOPB):
                slot = home[lists[k * QPER + i, t]]
                mine = (slot & 3) == z
                owner = slot >> 2
                b = ((owner & 1) ^ k) * NCHIP + (owner >> 1)
                ents[n] = (q << 15) | ((seen * NQ + q) << 5) | b
                step = mine.astype(jnp.int32)
                n = n + step
                seen = seen + step
            return n

        return lax.fori_loop(0, QPER, block, n)

    n = jnp.int32(0)
    for r, lists in enumerate((l0, l1, l2, l3)):
        n = group(r, lists, n)
    for u in range(8):
        ents[n + u] = (NQ << 15) | (NENT << 5)
    ents[COUNT] = n


def make_list(place, lists, home):
    smem = pl.BlockSpec(memory_space=pltpu.SMEM)
    return pl.pallas_call(
        list_kernel,
        out_shape=jax.ShapeDtypeStruct((COUNT + 8,), jnp.int32),
        in_specs=[smem] * 6,
        out_specs=smem,
        name="entry_list",
    )(place, *lists, home)


def fetch(qrefs, grefs, kvrefs, qs, gs, kv, sems):
    pairs = [(ref, kv.at[p]) for p, ref in enumerate(kvrefs)]
    pairs += [(ref.at[:QPER], qs.at[r]) for r, ref in enumerate(qrefs)]
    pairs += [(ref, gs.at[r]) for r, ref in enumerate(grefs)]
    copies = [pltpu.make_async_copy(a, b, sems.at[n]) for n, (a, b) in enumerate(pairs)]
    for copy in copies:
        copy.start()
    return copies


def unpack(p):
    q = p >> 15
    b = p & 31
    return (q >> 3) & 3, q & 7, q, (p >> 5) & 1023, b >> 4, b & 15


def fwd_kernel(ents, q0, q1, q2, q3, g0, g1, g2, g3, kva, kvb, out, qs, gs, kv, st, sems):
    copies = fetch((q0, q1, q2, q3), (g0, g1, g2, g3), (kva, kvb), qs, gs, kv, sems)
    st[0] = jnp.full((NENT + 8, DH), -1e30, F32)
    st[1] = jnp.zeros((NENT + 8, DH), F32)
    st[2] = jnp.zeros((NENT + 8, DH), F32)
    for copy in copies:
        copy.wait()

    def body(n, carry):
        parts = [unpack(ents[UNROLL_F * n + u]) for u in range(UNROLL_F)]
        scores = [dot(kv[p[4], p[5], :BLK], qs[p[0], p[1]], NT) * SCALE for p in parts]
        dprob = [dot(kv[p[4], p[5], BLK:], gs[p[0], p[1]], NT) for p in parts]
        highs = [jnp.max(x, axis=0, keepdims=True) for x in scores]
        expo = [jnp.exp(x - high) for x, high in zip(scores, highs)]
        for p, high, e, d in zip(parts, highs, expo, dprob):
            row = pl.ds(p[3], 1)
            st[0, row, :] = high
            st[1, row, :] = jnp.sum(e, axis=0, keepdims=True)
            st[2, row, :] = jnp.sum(e.astype(BF).astype(F32) * d, axis=0, keepdims=True)
        return carry

    lax.fori_loop(0, (ents[COUNT] + UNROLL_F - 1) // UNROLL_F, body, 0)
    high = st[0, 0:NQ]
    for e in range(1, TOPB):
        high = jnp.maximum(high, st[0, e * NQ : (e + 1) * NQ])
    total = jnp.zeros((NQ, DH), F32)
    prod = jnp.zeros((NQ, DH), F32)
    for e in range(TOPB):
        rows = slice(e * NQ, (e + 1) * NQ)
        weight = jnp.exp(st[0, rows] - high)
        total = total + weight * st[1, rows]
        prod = prod + weight * st[2, rows]
    out[0] = high
    out[1] = total
    out[2] = prod


def scratch_in():
    return [
        pltpu.VMEM((NZ, QPER, BLK, DH), BF),
        pltpu.VMEM((NZ, QPER, BLK, DH), BF),
        pltpu.VMEM((2, NCHIP, 2 * BLK, DH), BF),
    ]


def forward(ents, xparts, kvs):
    smem = pl.BlockSpec(memory_space=pltpu.SMEM)
    far = pl.BlockSpec(memory_space=pl.ANY)
    return pl.pallas_call(
        fwd_kernel,
        out_shape=jax.ShapeDtypeStruct((3, NQ, DH), F32),
        in_specs=[smem] + [far] * 10,
        out_specs=pl.BlockSpec(memory_space=pltpu.VMEM),
        scratch_shapes=scratch_in()
        + [pltpu.VMEM((3, NENT + 8, DH), F32), pltpu.SemaphoreType.DMA((NCOPY,))],
        compiler_params=pltpu.CompilerParams(vmem_limit_bytes=14 * MB),
        name="forward",
    )(ents, *xparts, *kvs)


def bwd_kernel(
    ents, s0, s1, s2, s3, q0, q1, q2, q3, g0, g1, g2, g3, kva, kvb,
    dq0, dq1, dq2, dq3, own, other,
    qs, gs, kv, dq, dkv, away, dqs, lse, delta, sems, outsems,
):
    copies = fetch((q0, q1, q2, q3), (g0, g1, g2, g3), (kva, kvb), qs, gs, kv, sems)

    def clear(i, carry):
        zero = jnp.zeros((BLK, DH), F32)
        dq[i] = zero
        dkv[i, :BLK] = zero
        dkv[i, BLK:] = zero
        return carry

    lax.fori_loop(0, NQ, clear, 0)
    for r in range(NZ):
        rows = slice(r * QPER, (r + 1) * QPER)
        parts = []
        for ref, shift in ((s0, 0), (s1, 1), (s2, 2), (s3, 3)):
            at = (r + shift) % NZ
            parts.append([ref[n, at * QPER : (at + 1) * QPER] for n in range(3)])
        high = jnp.maximum(
            jnp.maximum(parts[0][0], parts[1][0]), jnp.maximum(parts[2][0], parts[3][0])
        )
        total = jnp.zeros((QPER, DH), F32)
        prod = jnp.zeros((QPER, DH), F32)
        for part in parts:
            weight = jnp.exp(part[0] - high)
            total = total + weight * part[1]
            prod = prod + weight * part[2]
        lse[rows] = high + jnp.log(total)
        delta[rows] = prod / total
    for copy in copies:
        copy.wait()

    lse[NQ : NQ + 8] = jnp.full((8, DH), 1e30, F32)
    delta[NQ : NQ + 8] = jnp.zeros((8, DH), F32)

    def body(n, carry):
        parts = [unpack(ents[UNROLL_B * n + u]) for u in range(UNROLL_B)]
        keys = [kv[p[4], p[5], :BLK] for p in parts]
        quer = [qs[p[0], p[1]] for p in parts]
        grad = [gs[p[0], p[1]] for p in parts]
        scores = [dot(a, b, NT) * SCALE for a, b in zip(keys, quer)]
        dprob = [dot(kv[p[4], p[5], BLK:], b, NT) for p, b in zip(parts, grad)]
        probs = [jnp.exp(x - lse[pl.ds(p[2], 1), :]) for x, p in zip(scores, parts)]
        dscore = [
            (x * (d - delta[pl.ds(p[2], 1), :]) * SCALE).astype(BF)
            for x, d, p in zip(probs, dprob, parts)
        ]
        gv = [dot(x.astype(BF), b, NN) for x, b in zip(probs, grad)]
        gk = [dot(x, b, NN) for x, b in zip(dscore, quer)]
        gq = [dot(x, b, TN) for x, b in zip(dscore, keys)]
        for p, a, b, c in zip(parts, gv, gk, gq):
            at = p[4] * NCHIP + p[5]
            dkv[at, BLK:] += a
            dkv[at, :BLK] += b
            dq[p[0] * QPER + p[1]] += c
        return carry

    lax.fori_loop(0, (ents[COUNT] + UNROLL_B - 1) // UNROLL_B, body, 0)
    away[...] = dkv[NCHIP:].astype(BF)
    sends = [pltpu.make_async_copy(away, other, outsems.at[0])]
    sends[0].start()
    sends.append(pltpu.make_async_copy(dkv.at[:NCHIP], own, outsems.at[1]))
    sends.append(pltpu.make_async_copy(dq.at[:QPER], dq0, outsems.at[2]))
    sends[1].start()
    sends[2].start()
    dqs[...] = dq[QPER:].astype(BF)
    for r, ref in enumerate((dq1, dq2, dq3)):
        part = dqs.at[r * QPER : (r + 1) * QPER]
        sends.append(pltpu.make_async_copy(part, ref, outsems.at[3 + r]))
        sends[-1].start()
    for send in sends:
        send.wait()


def backward(ents, stats, xparts, kvs):
    smem = pl.BlockSpec(memory_space=pltpu.SMEM)
    vmem = pl.BlockSpec(memory_space=pltpu.VMEM)
    far = pl.BlockSpec(memory_space=pl.ANY)
    tile = (BLK, DH)
    outs = [jax.ShapeDtypeStruct((QPER,) + tile, F32)]
    outs += [jax.ShapeDtypeStruct((QPER,) + tile, BF)] * 3
    pair = (NCHIP, 2 * BLK, DH)
    outs += [jax.ShapeDtypeStruct(pair, F32), jax.ShapeDtypeStruct(pair, BF)]
    return pl.pallas_call(
        bwd_kernel,
        out_shape=tuple(outs),
        in_specs=[smem] + [vmem] * 4 + [far] * 10,
        out_specs=tuple([far] * 6),
        scratch_shapes=scratch_in()
        + [
            pltpu.VMEM((NQ,) + tile, F32),
            pltpu.VMEM((NB, 2 * BLK, DH), F32),
            pltpu.VMEM(pair, BF),
            pltpu.VMEM((NQ - QPER,) + tile, BF),
            pltpu.VMEM((NQ + 8, DH), F32),
            pltpu.VMEM((NQ + 8, DH), F32),
            pltpu.SemaphoreType.DMA((NCOPY,)),
            pltpu.SemaphoreType.DMA((6,)),
        ],
        compiler_params=pltpu.CompilerParams(vmem_limit_bytes=24 * MB),
        name="backward",
    )(ents, *stats, *xparts, *kvs)


def place_parts(z, parts, sems):
    copies = []
    for n, (r, ref, out) in enumerate(parts):
        rows = pl.ds(pl.multiple_of(((z + r) & 3) * BLK, BLK), BLK)
        copies.append(pltpu.make_async_copy(ref, out.at[rows], sems.at[n]))
    for copy in copies:
        copy.start()
    for copy in copies:
        copy.wait()


def near_kernel(place, k0, k1, k3, v0, v1, v3, outk, outv, sems):
    parts = [(0, k0, outk), (1, k1, outk), (3, k3, outk)]
    parts += [(0, v0, outv), (1, v1, outv), (3, v3, outv)]
    place_parts(place[0], parts, sems)


def far_kernel(place, k2, v2, ink, inv, outk, outv, sems):
    place_parts(place[0], [(2, k2, outk), (2, v2, outv)], sems)


def place_near(place, kparts, vparts):
    smem = pl.BlockSpec(memory_space=pltpu.SMEM)
    vmem = pl.BlockSpec(memory_space=pltpu.VMEM)
    far = pl.BlockSpec(memory_space=pl.ANY)
    shape = jax.ShapeDtypeStruct((NZ * BLK, H * DH), BF)
    return pl.pallas_call(
        near_kernel,
        out_shape=(shape, shape),
        in_specs=[smem] + [vmem] * 6,
        out_specs=(far, far),
        scratch_shapes=[pltpu.SemaphoreType.DMA((6,))],
        compiler_params=pltpu.CompilerParams(vmem_limit_bytes=16 * MB),
        name="place_near",
    )(place, *kparts, *vparts)


def place_far(place, near, k_far, v_far):
    smem = pl.BlockSpec(memory_space=pltpu.SMEM)
    vmem = pl.BlockSpec(memory_space=pltpu.VMEM)
    far = pl.BlockSpec(memory_space=pl.ANY)
    shape = jax.ShapeDtypeStruct((NZ * BLK, H * DH), BF)
    return pl.pallas_call(
        far_kernel,
        out_shape=(shape, shape),
        in_specs=[smem, vmem, vmem, far, far],
        out_specs=(far, far),
        scratch_shapes=[pltpu.SemaphoreType.DMA((2,))],
        input_output_aliases={3: 0, 4: 1},
        compiler_params=pltpu.CompilerParams(vmem_limit_bytes=16 * MB),
        name="place_far",
    )(place, k_far, v_far, *near)


def heads_first(array):
    return jnp.transpose(array.reshape(array.shape[0], H, DH), (1, 0, 2))


def rows_first(array):
    return jnp.transpose(array, (1, 0, 2)).reshape(array.shape[1], H * DH)


def per_device(queries, grad_out, mem_keys, mem_values, block_lists, block_home):
    z = lax.axis_index("dp")
    m = lax.axis_index("mem")
    c, k = m // 2, m % 2
    place = jnp.stack([z, c, k]).astype(jnp.int32)

    q_own, g_own, kv_cat = prepare(place, queries, grad_out, mem_keys, mem_values, block_lists)
    kv_cat, l_far = lax.optimization_barrier((kv_cat, over_z(block_lists, 2)))
    q_prev = over_z(q_own, 1)
    g_next = over_z(g_own, -1)
    g_prev = over_z(g_own, 1)
    q_next = over_z(q_own, -1)
    kv_own, q_prev, g_next, g_prev, q_next = lax.optimization_barrier(
        (plane_exchange(kv_cat), q_prev, g_next, g_prev, q_next)
    )
    q_far = over_z(q_prev, 1)
    g_far = over_z(g_next, -1)
    kvs = (kv_own, swap_cores(kv_own))
    l_prev = q_prev[QPER, :TOPB, :TOPB].astype(jnp.int32)
    l_next = q_next[QPER, :TOPB, :TOPB].astype(jnp.int32)
    ents = make_list(place, (block_lists, l_next, l_far, l_prev), block_home)
    xparts = (q_own, q_next, q_far, q_prev, g_own, g_next, g_far, g_prev)

    stat = forward(ents, xparts, kvs)
    stats = (stat, over_z(stat, 1), over_z(stat, 2), over_z(stat, -1))
    dq0, dq1, dq2, dq3, own, other = backward(ents, stats, xparts, kvs)

    both = (own + swap_cores(other).astype(F32)).astype(BF)
    got = plane_exchange(both)
    k_own, v_own = rows_first(got[:, :BLK]), rows_first(got[:, BLK:])
    v_prev = over_z(v_own, 1)
    v_next = over_z(v_own, -1)
    k_next = over_z(k_own, -1)
    k_prev = over_z(k_own, 1)
    v_far = over_z(v_prev, 1)
    k_far = over_z(k_next, -1)
    near = place_near(place, (k_own, k_next, k_prev), (v_own, v_next, v_prev))
    grad_keys, grad_values = place_far(place, near, k_far, v_far)

    dq_sum = (
        dq0
        + over_z(dq1, 1).astype(F32)
        + over_z(dq3, -1).astype(F32)
        + over_z(dq2, 2).astype(F32)
    ).astype(BF)
    half = BLK // 2
    keep = lax.dynamic_slice_in_dim(dq_sum, k * half, half, 1)
    give = lax.dynamic_slice_in_dim(dq_sum, (1 - k) * half, half, 1)
    got = swap_cores(give)
    whole = jnp.where(
        k == 0, jnp.concatenate([keep, got], axis=0), jnp.concatenate([got, keep], axis=0)
    )
    grad_queries = rows_first(plane_exchange(whole))
    return grad_queries, grad_keys, grad_values


def solution(mesh):
    in_specs = (P("dp", None), P("dp", None), P("mem", None), P("mem", None), P("dp", None), P())
    out_specs = (P(("dp", "mem"), None), P("mem", None), P("mem", None))
    return jax.shard_map(
        per_device, mesh=mesh, in_specs=in_specs, out_specs=out_specs, check_vma=False
    )
```

```python
import jax
import jax.numpy as jnp
from jax import lax
from jax.experimental import pallas as pl
from jax.experimental.pallas import tpu as pltpu
from jax.sharding import PartitionSpec as P

H = 16
DH = 128
BLK = 128
TOPB = 16
NZ = 4
NCHIP = 16
QPER = 8
NQ = NZ * QPER
NB = 2 * NCHIP
NENT = NQ * TOPB
COUNT = NENT + 8
NCOPY = 2 * NZ + 2
UNROLL_F = 8
UNROLL_B = 8
SCALE = DH ** (-0.5)
BF = jnp.bfloat16
F32 = jnp.float32
MB = 1 << 20


NT = (((1,), (1,)), ((), ()))
NN = (((1,), (0,)), ((), ()))
TN = (((0,), (0,)), ((), ()))


def dot(a, b, dims):
    return lax.dot_general(a, b, dims, preferred_element_type=F32)


def over_z(array, shift):
    return lax.ppermute(array, "dp", [(i, (i + shift) % NZ) for i in range(NZ)])


def swap_cores(array):
    return lax.ppermute(array, "mem", [(i, i ^ 1) for i in range(2 * NCHIP)])


def plane_exchange(array):
    groups = [[2 * c + k for c in range(NCHIP)] for k in range(2)]
    return lax.all_to_all(array, "mem", 0, 0, axis_index_groups=groups)


def prepare_kernel(place, queries, grads, keys, values, q, g, kv, sems):
    z, c, k = place[0], place[1], place[2]
    cols = pl.ds(pl.multiple_of(c * DH, DH), DH)
    pairs = []
    for i in range(QPER):
        rows = pl.ds(pl.multiple_of((k * QPER + i) * BLK, BLK), BLK)
        pairs.append((queries.at[rows, cols], q.at[i]))
        pairs.append((grads.at[rows, cols], g.at[i]))
    rows = pl.ds(pl.multiple_of(z * BLK, BLK), BLK)
    for h in range(H):
        cols = slice(h * DH, (h + 1) * DH)
        pairs.append((keys.at[rows, cols], kv.at[h, :BLK]))
        pairs.append((values.at[rows, cols], kv.at[h, BLK:]))
    copies = [pltpu.make_async_copy(a, b, sems.at[n]) for n, (a, b) in enumerate(pairs)]
    for copy in copies:
        copy.start()
    for copy in copies:
        copy.wait()


def prepare(place, queries, grads, keys, values):
    smem = pl.BlockSpec(memory_space=pltpu.SMEM)
    vmem = pl.BlockSpec(memory_space=pltpu.VMEM)
    far = pl.BlockSpec(memory_space=pl.ANY)
    return pl.pallas_call(
        prepare_kernel,
        out_shape=(
            jax.ShapeDtypeStruct((QPER, BLK, DH), BF),
            jax.ShapeDtypeStruct((QPER, BLK, DH), BF),
            jax.ShapeDtypeStruct((H, 2 * BLK, DH), BF),
        ),
        in_specs=[smem] + [far] * 4,
        out_specs=(vmem, vmem, vmem),
        scratch_shapes=[pltpu.SemaphoreType.DMA((2 * QPER + 2 * H,))],
        compiler_params=pltpu.CompilerParams(vmem_limit_bytes=60 * MB),
        name="prepare",
    )(place, queries, grads, keys, values)


def list_kernel(place, l0, l1, l2, l3, home, ents):
    z = place[0]
    k = place[2]

    def group(r, lists, n):
        def block(i, n):
            q = r * QPER + i
            seen = jnp.int32(0)
            for t in range(TOPB):
                slot = home[lists[k * QPER + i, t]]
                mine = (slot & 3) == z
                owner = slot >> 2
                b = ((owner & 1) ^ k) * NCHIP + (owner >> 1)
                ents[n] = (q << 15) | ((seen * NQ + q) << 5) | b
                step = mine.astype(jnp.int32)
                n = n + step
                seen = seen + step
            return n

        return lax.fori_loop(0, QPER, block, n)

    n = jnp.int32(0)
    for r, lists in enumerate((l0, l1, l2, l3)):
        n = group(r, lists, n)
    for u in range(8):
        ents[n + u] = (NQ << 15) | (NENT << 5)
    ents[COUNT] = n


def make_list(place, lists, home):
    smem = pl.BlockSpec(memory_space=pltpu.SMEM)
    return pl.pallas_call(
        list_kernel,
        out_shape=jax.ShapeDtypeStruct((COUNT + 8,), jnp.int32),
        in_specs=[smem] * 6,
        out_specs=smem,
        compiler_params=pltpu.CompilerParams(vmem_limit_bytes=MB),
        name="entry_list",
    )(place, *lists, home)


def fetch(qrefs, grefs, kvrefs, qs, gs, kv, sems):
    pairs = [(ref, kv.at[p]) for p, ref in enumerate(kvrefs)]
    pairs += [(ref, qs.at[r]) for r, ref in enumerate(qrefs)]
    pairs += [(ref, gs.at[r]) for r, ref in enumerate(grefs)]
    copies = [pltpu.make_async_copy(a, b, sems.at[n]) for n, (a, b) in enumerate(pairs)]
    for copy in copies:
        copy.start()
    return copies


def unpack(p):
    q = p >> 15
    b = p & 31
    return (q >> 3) & 3, q & 7, q, (p >> 5) & 1023, b >> 4, b & 15


def fwd_kernel(ents, q0, q1, q2, q3, g0, g1, g2, g3, kva, kvb, out, qs, gs, kv, st, sems):
    copies = fetch((q0, q1, q2, q3), (g0, g1, g2, g3), (kva, kvb), qs, gs, kv, sems)
    st[0] = jnp.full((NENT + 8, DH), -1e30, F32)
    st[1] = jnp.zeros((NENT + 8, DH), F32)
    st[2] = jnp.zeros((NENT + 8, DH), F32)
    for copy in copies:
        copy.wait()

    def body(n, carry):
        parts = [unpack(ents[UNROLL_F * n + u]) for u in range(UNROLL_F)]
        scores = [dot(kv[p[4], p[5], :BLK], qs[p[0], p[1]], NT) * SCALE for p in parts]
        dprob = [dot(kv[p[4], p[5], BLK:], gs[p[0], p[1]], NT) for p in parts]
        highs = [jnp.max(x, axis=0, keepdims=True) for x in scores]
        expo = [jnp.exp(x - high) for x, high in zip(scores, highs)]
        for p, high, e, d in zip(parts, highs, expo, dprob):
            row = pl.ds(p[3], 1)
            st[0, row, :] = high
            st[1, row, :] = jnp.sum(e, axis=0, keepdims=True)
            st[2, row, :] = jnp.sum(e.astype(BF).astype(F32) * d, axis=0, keepdims=True)
        return carry

    lax.fori_loop(0, (ents[COUNT] + UNROLL_F - 1) // UNROLL_F, body, 0)
    high = st[0, 0:NQ]
    for e in range(1, TOPB):
        high = jnp.maximum(high, st[0, e * NQ : (e + 1) * NQ])
    total = jnp.zeros((NQ, DH), F32)
    prod = jnp.zeros((NQ, DH), F32)
    for e in range(TOPB):
        rows = slice(e * NQ, (e + 1) * NQ)
        weight = jnp.exp(st[0, rows] - high)
        total = total + weight * st[1, rows]
        prod = prod + weight * st[2, rows]
    out[0] = high
    out[1] = total
    out[2] = prod


def scratch_in():
    return [
        pltpu.VMEM((NZ, QPER, BLK, DH), BF),
        pltpu.VMEM((NZ, QPER, BLK, DH), BF),
        pltpu.VMEM((2, NCHIP, 2 * BLK, DH), BF),
    ]


def forward(ents, xparts, kvs):
    smem = pl.BlockSpec(memory_space=pltpu.SMEM)
    far = pl.BlockSpec(memory_space=pl.ANY)
    return pl.pallas_call(
        fwd_kernel,
        out_shape=jax.ShapeDtypeStruct((3, NQ, DH), F32),
        in_specs=[smem] + [far] * 10,
        out_specs=pl.BlockSpec(memory_space=pltpu.VMEM),
        scratch_shapes=scratch_in()
        + [pltpu.VMEM((3, NENT + 8, DH), F32), pltpu.SemaphoreType.DMA((NCOPY,))],
        compiler_params=pltpu.CompilerParams(vmem_limit_bytes=14 * MB),
        name="forward",
    )(ents, *xparts, *kvs)


def bwd_kernel(
    ents, s0, s1, s2, s3, q0, q1, q2, q3, g0, g1, g2, g3, kva, kvb,
    dq0, dq1, dq2, dq3, own, other,
    qs, gs, kv, dq, dkv, away, dqs, lse, delta, sems, outsems,
):
    copies = fetch((q0, q1, q2, q3), (g0, g1, g2, g3), (kva, kvb), qs, gs, kv, sems)

    def clear(i, carry):
        zero = jnp.zeros((BLK, DH), F32)
        dq[i] = zero
        dkv[i, :BLK] = zero
        dkv[i, BLK:] = zero
        return carry

    lax.fori_loop(0, NQ, clear, 0)
    for r in range(NZ):
        rows = slice(r * QPER, (r + 1) * QPER)
        parts = []
        for ref, shift in ((s0, 0), (s1, 1), (s2, 2), (s3, 3)):
            at = (r + shift) % NZ
            parts.append([ref[n, at * QPER : (at + 1) * QPER] for n in range(3)])
        high = jnp.maximum(
            jnp.maximum(parts[0][0], parts[1][0]), jnp.maximum(parts[2][0], parts[3][0])
        )
        total = jnp.zeros((QPER, DH), F32)
        prod = jnp.zeros((QPER, DH), F32)
        for part in parts:
            weight = jnp.exp(part[0] - high)
            total = total + weight * part[1]
            prod = prod + weight * part[2]
        lse[rows] = high + jnp.log(total)
        delta[rows] = prod / total
    for copy in copies:
        copy.wait()

    lse[NQ : NQ + 8] = jnp.full((8, DH), 1e30, F32)
    delta[NQ : NQ + 8] = jnp.zeros((8, DH), F32)

    def body(n, carry):
        parts = [unpack(ents[UNROLL_B * n + u]) for u in range(UNROLL_B)]
        keys = [kv[p[4], p[5], :BLK] for p in parts]
        quer = [qs[p[0], p[1]] for p in parts]
        grad = [gs[p[0], p[1]] for p in parts]
        scores = [dot(a, b, NT) * SCALE for a, b in zip(keys, quer)]
        dprob = [dot(kv[p[4], p[5], BLK:], b, NT) for p, b in zip(parts, grad)]
        probs = [jnp.exp(x - lse[pl.ds(p[2], 1), :]) for x, p in zip(scores, parts)]
        dscore = [
            (x * (d - delta[pl.ds(p[2], 1), :]) * SCALE).astype(BF)
            for x, d, p in zip(probs, dprob, parts)
        ]
        gv = [dot(x.astype(BF), b, NN) for x, b in zip(probs, grad)]
        gk = [dot(x, b, NN) for x, b in zip(dscore, quer)]
        gq = [dot(x, b, TN) for x, b in zip(dscore, keys)]
        for p, a, b, c in zip(parts, gv, gk, gq):
            at = p[4] * NCHIP + p[5]
            dkv[at, BLK:] += a
            dkv[at, :BLK] += b
            dq[p[0] * QPER + p[1]] += c
        return carry

    lax.fori_loop(0, (ents[COUNT] + UNROLL_B - 1) // UNROLL_B, body, 0)
    away[...] = dkv[NCHIP:].astype(BF)
    sends = [pltpu.make_async_copy(away, other, outsems.at[0])]
    sends[0].start()
    sends.append(pltpu.make_async_copy(dkv.at[:NCHIP], own, outsems.at[1]))
    sends.append(pltpu.make_async_copy(dq.at[:QPER], dq0, outsems.at[2]))
    sends[1].start()
    sends[2].start()
    dqs[...] = dq[QPER:].astype(BF)
    for r, ref in enumerate((dq1, dq2, dq3)):
        part = dqs.at[r * QPER : (r + 1) * QPER]
        sends.append(pltpu.make_async_copy(part, ref, outsems.at[3 + r]))
        sends[-1].start()
    for send in sends:
        send.wait()


def backward(ents, stats, xparts, kvs):
    smem = pl.BlockSpec(memory_space=pltpu.SMEM)
    vmem = pl.BlockSpec(memory_space=pltpu.VMEM)
    far = pl.BlockSpec(memory_space=pl.ANY)
    tile = (BLK, DH)
    outs = [jax.ShapeDtypeStruct((QPER,) + tile, F32)]
    outs += [jax.ShapeDtypeStruct((QPER,) + tile, BF)] * 3
    pair = (NCHIP, 2 * BLK, DH)
    outs += [jax.ShapeDtypeStruct(pair, F32), jax.ShapeDtypeStruct(pair, BF)]
    return pl.pallas_call(
        bwd_kernel,
        out_shape=tuple(outs),
        in_specs=[smem] + [vmem] * 4 + [far] * 10,
        out_specs=tuple([far] * 6),
        scratch_shapes=scratch_in()
        + [
            pltpu.VMEM((NQ,) + tile, F32),
            pltpu.VMEM((NB, 2 * BLK, DH), F32),
            pltpu.VMEM(pair, BF),
            pltpu.VMEM((NQ - QPER,) + tile, BF),
            pltpu.VMEM((NQ + 8, DH), F32),
            pltpu.VMEM((NQ + 8, DH), F32),
            pltpu.SemaphoreType.DMA((NCOPY,)),
            pltpu.SemaphoreType.DMA((6,)),
        ],
        compiler_params=pltpu.CompilerParams(vmem_limit_bytes=24 * MB),
        name="backward",
    )(ents, *stats, *xparts, *kvs)


def place_parts(z, parts, sems):
    copies = []
    for n, (r, ref, out) in enumerate(parts):
        rows = pl.ds(pl.multiple_of(((z + r) & 3) * BLK, BLK), BLK)
        copies.append(pltpu.make_async_copy(ref, out.at[rows], sems.at[n]))
    for copy in copies:
        copy.start()
    for copy in copies:
        copy.wait()


def near_kernel(place, k0, k1, k3, v0, v1, v3, outk, outv, sems):
    parts = [(0, k0, outk), (1, k1, outk), (3, k3, outk)]
    parts += [(0, v0, outv), (1, v1, outv), (3, v3, outv)]
    place_parts(place[0], parts, sems)


def far_kernel(place, k2, v2, ink, inv, outk, outv, sems):
    place_parts(place[0], [(2, k2, outk), (2, v2, outv)], sems)


def place_near(place, kparts, vparts):
    smem = pl.BlockSpec(memory_space=pltpu.SMEM)
    vmem = pl.BlockSpec(memory_space=pltpu.VMEM)
    far = pl.BlockSpec(memory_space=pl.ANY)
    shape = jax.ShapeDtypeStruct((NZ * BLK, H * DH), BF)
    return pl.pallas_call(
        near_kernel,
        out_shape=(shape, shape),
        in_specs=[smem] + [vmem] * 6,
        out_specs=(far, far),
        scratch_shapes=[pltpu.SemaphoreType.DMA((6,))],
        compiler_params=pltpu.CompilerParams(vmem_limit_bytes=8 * MB),
        name="place_near",
    )(place, *kparts, *vparts)


def place_far(place, near, k_far, v_far):
    smem = pl.BlockSpec(memory_space=pltpu.SMEM)
    vmem = pl.BlockSpec(memory_space=pltpu.VMEM)
    far = pl.BlockSpec(memory_space=pl.ANY)
    shape = jax.ShapeDtypeStruct((NZ * BLK, H * DH), BF)
    return pl.pallas_call(
        far_kernel,
        out_shape=(shape, shape),
        in_specs=[smem, vmem, vmem, far, far],
        out_specs=(far, far),
        scratch_shapes=[pltpu.SemaphoreType.DMA((2,))],
        input_output_aliases={3: 0, 4: 1},
        compiler_params=pltpu.CompilerParams(vmem_limit_bytes=8 * MB),
        name="place_far",
    )(place, k_far, v_far, *near)


def heads_first(array):
    return jnp.transpose(array.reshape(array.shape[0], H, DH), (1, 0, 2))


def rows_first(array):
    return jnp.transpose(array, (1, 0, 2)).reshape(array.shape[1], H * DH)


def per_device(queries, grad_out, mem_keys, mem_values, block_lists, block_home):
    z = lax.axis_index("dp")
    m = lax.axis_index("mem")
    c, k = m // 2, m % 2
    place = jnp.stack([z, c, k]).astype(jnp.int32)

    q_own, g_own, kv_cat = prepare(place, queries, grad_out, mem_keys, mem_values)
    lists = tuple(over_z(block_lists, shift) for shift in (-1, 2, 1))
    kv_cat, lists = lax.optimization_barrier((kv_cat, lists))
    ents = make_list(place, (block_lists,) + lists, block_home)
    q_prev = over_z(q_own, 1)
    g_next = over_z(g_own, -1)
    g_prev = over_z(g_own, 1)
    q_next = over_z(q_own, -1)
    kv_own, q_prev, g_next, g_prev, q_next, ents = lax.optimization_barrier(
        (plane_exchange(kv_cat), q_prev, g_next, g_prev, q_next, ents)
    )
    q_far = over_z(q_prev, 1)
    g_far = over_z(g_next, -1)
    kvs = (kv_own, swap_cores(kv_own))
    xparts = (q_own, q_next, q_far, q_prev, g_own, g_next, g_far, g_prev)

    stat = forward(ents, xparts, kvs)
    stats = (stat, over_z(stat, 1), over_z(stat, 2), over_z(stat, -1))
    dq0, dq1, dq2, dq3, own, other = backward(ents, stats, xparts, kvs)

    both = (own + swap_cores(other).astype(F32)).astype(BF)
    got = plane_exchange(both)
    k_own, v_own = rows_first(got[:, :BLK]), rows_first(got[:, BLK:])
    v_prev = over_z(v_own, 1)
    v_next = over_z(v_own, -1)
    k_next = over_z(k_own, -1)
    k_prev = over_z(k_own, 1)
    dq_sum = (
        dq0
        + over_z(dq1, 1).astype(F32)
        + over_z(dq3, -1).astype(F32)
        + over_z(dq2, 2).astype(F32)
    ).astype(BF)
    half = BLK // 2
    keep = lax.dynamic_slice_in_dim(dq_sum, k * half, half, 1)
    give = lax.dynamic_slice_in_dim(dq_sum, (1 - k) * half, half, 1)
    got = swap_cores(give)
    whole = jnp.where(
        k == 0, jnp.concatenate([keep, got], axis=0), jnp.concatenate([got, keep], axis=0)
    )
    whole, v_prev, k_next = lax.optimization_barrier((whole, v_prev, k_next))
    v_far = over_z(v_prev, 1)
    k_far = over_z(k_next, -1)
    near = place_near(place, (k_own, k_next, k_prev), (v_own, v_next, v_prev))
    grad_keys, grad_values = place_far(place, near, k_far, v_far)
    grad_queries = rows_first(plane_exchange(whole))
    return grad_queries, grad_keys, grad_values


def solution(mesh):
    in_specs = (P("dp", None), P("dp", None), P("mem", None), P("mem", None), P("dp", None), P())
    out_specs = (P(("dp", "mem"), None), P("mem", None), P("mem", None))
    return jax.shard_map(
        per_device, mesh=mesh, in_specs=in_specs, out_specs=out_specs, check_vma=False
    )
```

```python
import functools

import jax
import jax.numpy as jnp
from jax import lax
from jax.experimental import pallas as pl
from jax.experimental.pallas import tpu as pltpu
from jax.sharding import PartitionSpec as P

H = 16
DH = 128
BLK = 128
TOPB = 16
NZ = 4
NCHIP = 16
QPER = 8
NQ = NZ * QPER
NB = 2 * NCHIP
NENT = NQ * TOPB
EARLY = (0, 1, 3)
LATE = (2,)
LATE_AT = len(EARLY) * QPER * TOPB + 8
COUNT = LATE_AT + len(LATE) * QPER * TOPB + 8
NCOPY = 2 * NZ + 2
UNROLL_F = 8
UNROLL_B = 8
SCALE = DH ** (-0.5)
BF = jnp.bfloat16
F32 = jnp.float32
MB = 1 << 20


NT = (((1,), (1,)), ((), ()))
NN = (((1,), (0,)), ((), ()))
TN = (((0,), (0,)), ((), ()))


def dot(a, b, dims):
    return lax.dot_general(a, b, dims, preferred_element_type=F32)


def over_z(array, shift):
    return lax.ppermute(array, "dp", [(i, (i + shift) % NZ) for i in range(NZ)])


def swap_cores(array):
    return lax.ppermute(array, "mem", [(i, i ^ 1) for i in range(2 * NCHIP)])


def plane_exchange(array):
    groups = [[2 * c + k for c in range(NCHIP)] for k in range(2)]
    return lax.all_to_all(array, "mem", 0, 0, axis_index_groups=groups)


def prepare_kernel(place, queries, grads, keys, values, q, g, kv, sems):
    z, c, k = place[0], place[1], place[2]
    cols = pl.ds(pl.multiple_of(c * DH, DH), DH)
    pairs = []
    for i in range(QPER):
        rows = pl.ds(pl.multiple_of((k * QPER + i) * BLK, BLK), BLK)
        pairs.append((queries.at[rows, cols], q.at[i]))
        pairs.append((grads.at[rows, cols], g.at[i]))
    rows = pl.ds(pl.multiple_of(z * BLK, BLK), BLK)
    for h in range(H):
        cols = slice(h * DH, (h + 1) * DH)
        pairs.append((keys.at[rows, cols], kv.at[h, :BLK]))
        pairs.append((values.at[rows, cols], kv.at[h, BLK:]))
    copies = [pltpu.make_async_copy(a, b, sems.at[n]) for n, (a, b) in enumerate(pairs)]
    for copy in copies:
        copy.start()
    for copy in copies:
        copy.wait()


def prepare(place, queries, grads, keys, values):
    smem = pl.BlockSpec(memory_space=pltpu.SMEM)
    vmem = pl.BlockSpec(memory_space=pltpu.VMEM)
    far = pl.BlockSpec(memory_space=pl.ANY)
    return pl.pallas_call(
        prepare_kernel,
        out_shape=(
            jax.ShapeDtypeStruct((QPER, BLK, DH), BF),
            jax.ShapeDtypeStruct((QPER, BLK, DH), BF),
            jax.ShapeDtypeStruct((H, 2 * BLK, DH), BF),
        ),
        in_specs=[smem] + [far] * 4,
        out_specs=(vmem, vmem, vmem),
        scratch_shapes=[pltpu.SemaphoreType.DMA((2 * QPER + 2 * H,))],
        compiler_params=pltpu.CompilerParams(vmem_limit_bytes=60 * MB),
        name="prepare",
    )(place, queries, grads, keys, values)


def list_kernel(place, l0, l1, l2, l3, home, ents):
    z = place[0]
    k = place[2]

    def group(r, lists, n):
        def block(i, n):
            q = r * QPER + i
            seen = jnp.int32(0)
            for t in range(TOPB):
                slot = home[lists[k * QPER + i, t]]
                mine = (slot & 3) == z
                owner = slot >> 2
                b = ((owner & 1) ^ k) * NCHIP + (owner >> 1)
                ents[n] = (q << 15) | ((seen * NQ + q) << 5) | b
                step = mine.astype(jnp.int32)
                n = n + step
                seen = seen + step
            return n

        return lax.fori_loop(0, QPER, block, n)

    every = (l0, l1, l2, l3)
    for part, (start, groups) in enumerate(((0, EARLY), (LATE_AT, LATE))):
        n = jnp.int32(start)
        for r in groups:
            n = group(r, every[r], n)
        for u in range(8):
            ents[n + u] = ((NQ + groups[0] * QPER) << 15) | (NENT << 5)
        ents[COUNT + part] = n - start


def make_list(place, lists, home):
    smem = pl.BlockSpec(memory_space=pltpu.SMEM)
    return pl.pallas_call(
        list_kernel,
        out_shape=jax.ShapeDtypeStruct((COUNT + 8,), jnp.int32),
        in_specs=[smem] * 6,
        out_specs=smem,
        compiler_params=pltpu.CompilerParams(vmem_limit_bytes=MB),
        name="entry_list",
    )(place, *lists, home)


def fetch(groups, qrefs, grefs, kvrefs, qs, gs, kv, sems):
    pairs = [(ref, kv.at[p]) for p, ref in enumerate(kvrefs)]
    pairs += [(ref, qs.at[r]) for r, ref in zip(groups, qrefs)]
    pairs += [(ref, gs.at[r]) for r, ref in zip(groups, grefs)]
    copies = [pltpu.make_async_copy(a, b, sems.at[n]) for n, (a, b) in enumerate(pairs)]
    for copy in copies:
        copy.start()
    return copies


def unpack(p):
    q = p >> 15
    b = p & 31
    return (q >> 3) & 3, q & 7, q, (p >> 5) & 1023, b >> 4, b & 15


def fwd_kernel(groups, start, ents, before, *refs):
    size = len(groups)
    out, qs, gs, kv, st, sems = refs[2 * size + 2 :]
    copies = fetch(
        groups, refs[:size], refs[size : 2 * size], refs[2 * size : 2 * size + 2], qs, gs, kv, sems
    )
    st[0] = jnp.full((NENT + 8, DH), -1e30, F32)
    st[1] = jnp.zeros((NENT + 8, DH), F32)
    st[2] = jnp.zeros((NENT + 8, DH), F32)
    for copy in copies:
        copy.wait()

    def body(n, carry):
        parts = [unpack(ents[start + UNROLL_F * n + u]) for u in range(UNROLL_F)]
        scores = [dot(kv[p[4], p[5], :BLK], qs[p[0], p[1]], NT) * SCALE for p in parts]
        dprob = [dot(kv[p[4], p[5], BLK:], gs[p[0], p[1]], NT) for p in parts]
        highs = [jnp.max(x, axis=0, keepdims=True) for x in scores]
        expo = [jnp.exp(x - high) for x, high in zip(scores, highs)]
        for p, high, e, d in zip(parts, highs, expo, dprob):
            row = pl.ds(p[3], 1)
            st[0, row, :] = high
            st[1, row, :] = jnp.sum(e, axis=0, keepdims=True)
            st[2, row, :] = jnp.sum(e.astype(BF).astype(F32) * d, axis=0, keepdims=True)
        return carry

    part = 0 if start == 0 else 1
    lax.fori_loop(0, (ents[COUNT + part] + UNROLL_F - 1) // UNROLL_F, body, 0)
    out[...] = before[...]
    for r in groups:
        rows = [slice(e * NQ + r * QPER, e * NQ + (r + 1) * QPER) for e in range(TOPB)]
        high = st[0, rows[0]]
        for row in rows[1:]:
            high = jnp.maximum(high, st[0, row])
        total = jnp.zeros((QPER, DH), F32)
        prod = jnp.zeros((QPER, DH), F32)
        for row in rows:
            weight = jnp.exp(st[0, row] - high)
            total = total + weight * st[1, row]
            prod = prod + weight * st[2, row]
        at = slice(r * QPER, (r + 1) * QPER)
        out[0, at] = high
        out[1, at] = total
        out[2, at] = prod


def scratch_in():
    return [
        pltpu.VMEM((NZ, QPER, BLK, DH), BF),
        pltpu.VMEM((NZ, QPER, BLK, DH), BF),
        pltpu.VMEM((2, NCHIP, 2 * BLK, DH), BF),
    ]


def forward(groups, start, ents, before, qparts, gparts, kvs):
    smem = pl.BlockSpec(memory_space=pltpu.SMEM)
    vmem = pl.BlockSpec(memory_space=pltpu.VMEM)
    far = pl.BlockSpec(memory_space=pl.ANY)
    return pl.pallas_call(
        functools.partial(fwd_kernel, groups, start),
        out_shape=jax.ShapeDtypeStruct((3, NQ, DH), F32),
        in_specs=[smem, vmem] + [far] * (2 * len(groups) + 2),
        out_specs=vmem,
        scratch_shapes=scratch_in()
        + [pltpu.VMEM((3, NENT + 8, DH), F32), pltpu.SemaphoreType.DMA((NCOPY,))],
        compiler_params=pltpu.CompilerParams(vmem_limit_bytes=14 * MB),
        name="forward",
    )(ents, before, *qparts, *gparts, *kvs)


def bwd_kernel(
    ents, s0, s1, s2, s3, q0, q1, q2, q3, g0, g1, g2, g3, kva, kvb,
    dq0, dq1, dq2, dq3, own, other,
    qs, gs, kv, dq, dkv, away, dqs, lse, delta, sems, outsems,
):
    copies = fetch(range(NZ), (q0, q1, q2, q3), (g0, g1, g2, g3), (kva, kvb), qs, gs, kv, sems)

    def clear(i, carry):
        zero = jnp.zeros((BLK, DH), F32)
        dq[i] = zero
        dkv[i, :BLK] = zero
        dkv[i, BLK:] = zero
        return carry

    lax.fori_loop(0, NQ, clear, 0)
    for r in range(NZ):
        rows = slice(r * QPER, (r + 1) * QPER)
        parts = []
        for ref, shift in ((s0, 0), (s1, 1), (s2, 2), (s3, 3)):
            at = (r + shift) % NZ
            parts.append([ref[n, at * QPER : (at + 1) * QPER] for n in range(3)])
        high = jnp.maximum(
            jnp.maximum(parts[0][0], parts[1][0]), jnp.maximum(parts[2][0], parts[3][0])
        )
        total = jnp.zeros((QPER, DH), F32)
        prod = jnp.zeros((QPER, DH), F32)
        for part in parts:
            weight = jnp.exp(part[0] - high)
            total = total + weight * part[1]
            prod = prod + weight * part[2]
        lse[rows] = high + jnp.log(total)
        delta[rows] = prod / total
    for copy in copies:
        copy.wait()

    lse[NQ:] = jnp.full((NQ, DH), 1e30, F32)
    delta[NQ:] = jnp.zeros((NQ, DH), F32)

    early = (ents[COUNT] + UNROLL_B - 1) // UNROLL_B
    late = (ents[COUNT + 1] + UNROLL_B - 1) // UNROLL_B

    def body(n, carry):
        at = jnp.where(n < early, n * UNROLL_B, LATE_AT + (n - early) * UNROLL_B)
        parts = [unpack(ents[at + u]) for u in range(UNROLL_B)]
        keys = [kv[p[4], p[5], :BLK] for p in parts]
        quer = [qs[p[0], p[1]] for p in parts]
        grad = [gs[p[0], p[1]] for p in parts]
        scores = [dot(a, b, NT) * SCALE for a, b in zip(keys, quer)]
        dprob = [dot(kv[p[4], p[5], BLK:], b, NT) for p, b in zip(parts, grad)]
        probs = [jnp.exp(x - lse[pl.ds(p[2], 1), :]) for x, p in zip(scores, parts)]
        dscore = [
            (x * (d - delta[pl.ds(p[2], 1), :]) * SCALE).astype(BF)
            for x, d, p in zip(probs, dprob, parts)
        ]
        gv = [dot(x.astype(BF), b, NN) for x, b in zip(probs, grad)]
        gk = [dot(x, b, NN) for x, b in zip(dscore, quer)]
        gq = [dot(x, b, TN) for x, b in zip(dscore, keys)]
        for p, a, b, c in zip(parts, gv, gk, gq):
            at = p[4] * NCHIP + p[5]
            dkv[at, BLK:] += a
            dkv[at, :BLK] += b
            dq[p[0] * QPER + p[1]] += c
        return carry

    lax.fori_loop(0, early + late, body, 0)
    away[...] = dkv[NCHIP:].astype(BF)
    sends = [pltpu.make_async_copy(away, other, outsems.at[0])]
    sends[0].start()
    sends.append(pltpu.make_async_copy(dkv.at[:NCHIP], own, outsems.at[1]))
    sends.append(pltpu.make_async_copy(dq.at[:QPER], dq0, outsems.at[2]))
    sends[1].start()
    sends[2].start()
    dqs[...] = dq[QPER:].astype(BF)
    for r, ref in enumerate((dq1, dq2, dq3)):
        part = dqs.at[r * QPER : (r + 1) * QPER]
        sends.append(pltpu.make_async_copy(part, ref, outsems.at[3 + r]))
        sends[-1].start()
    for send in sends:
        send.wait()


def backward(ents, stats, xparts, kvs):
    smem = pl.BlockSpec(memory_space=pltpu.SMEM)
    vmem = pl.BlockSpec(memory_space=pltpu.VMEM)
    far = pl.BlockSpec(memory_space=pl.ANY)
    tile = (BLK, DH)
    outs = [jax.ShapeDtypeStruct((QPER,) + tile, F32)]
    outs += [jax.ShapeDtypeStruct((QPER,) + tile, BF)] * 3
    pair = (NCHIP, 2 * BLK, DH)
    outs += [jax.ShapeDtypeStruct(pair, F32), jax.ShapeDtypeStruct(pair, BF)]
    return pl.pallas_call(
        bwd_kernel,
        out_shape=tuple(outs),
        in_specs=[smem] + [vmem] * 4 + [far] * 10,
        out_specs=tuple([far] * 6),
        scratch_shapes=scratch_in()
        + [
            pltpu.VMEM((NQ,) + tile, F32),
            pltpu.VMEM((NB, 2 * BLK, DH), F32),
            pltpu.VMEM(pair, BF),
            pltpu.VMEM((NQ - QPER,) + tile, BF),
            pltpu.VMEM((2 * NQ, DH), F32),
            pltpu.VMEM((2 * NQ, DH), F32),
            pltpu.SemaphoreType.DMA((NCOPY,)),
            pltpu.SemaphoreType.DMA((6,)),
        ],
        compiler_params=pltpu.CompilerParams(vmem_limit_bytes=24 * MB),
        name="backward",
    )(ents, *stats, *xparts, *kvs)


def place_parts(z, parts, sems):
    copies = []
    for n, (r, ref, out) in enumerate(parts):
        rows = pl.ds(pl.multiple_of(((z + r) & 3) * BLK, BLK), BLK)
        copies.append(pltpu.make_async_copy(ref, out.at[rows], sems.at[n]))
    for copy in copies:
        copy.start()
    for copy in copies:
        copy.wait()


def near_kernel(place, k0, k1, k3, v0, v1, v3, outk, outv, sems):
    parts = [(0, k0, outk), (1, k1, outk), (3, k3, outk)]
    parts += [(0, v0, outv), (1, v1, outv), (3, v3, outv)]
    place_parts(place[0], parts, sems)


def far_kernel(place, k2, v2, ink, inv, outk, outv, sems):
    place_parts(place[0], [(2, k2, outk), (2, v2, outv)], sems)


def place_near(place, kparts, vparts):
    smem = pl.BlockSpec(memory_space=pltpu.SMEM)
    vmem = pl.BlockSpec(memory_space=pltpu.VMEM)
    far = pl.BlockSpec(memory_space=pl.ANY)
    shape = jax.ShapeDtypeStruct((NZ * BLK, H * DH), BF)
    return pl.pallas_call(
        near_kernel,
        out_shape=(shape, shape),
        in_specs=[smem] + [vmem] * 6,
        out_specs=(far, far),
        scratch_shapes=[pltpu.SemaphoreType.DMA((6,))],
        compiler_params=pltpu.CompilerParams(vmem_limit_bytes=8 * MB),
        name="place_near",
    )(place, *kparts, *vparts)


def place_far(place, near, k_far, v_far):
    smem = pl.BlockSpec(memory_space=pltpu.SMEM)
    vmem = pl.BlockSpec(memory_space=pltpu.VMEM)
    far = pl.BlockSpec(memory_space=pl.ANY)
    shape = jax.ShapeDtypeStruct((NZ * BLK, H * DH), BF)
    return pl.pallas_call(
        far_kernel,
        out_shape=(shape, shape),
        in_specs=[smem, vmem, vmem, far, far],
        out_specs=(far, far),
        scratch_shapes=[pltpu.SemaphoreType.DMA((2,))],
        input_output_aliases={3: 0, 4: 1},
        compiler_params=pltpu.CompilerParams(vmem_limit_bytes=8 * MB),
        name="place_far",
    )(place, k_far, v_far, *near)


def heads_first(array):
    return jnp.transpose(array.reshape(array.shape[0], H, DH), (1, 0, 2))


def rows_first(array):
    return jnp.transpose(array, (1, 0, 2)).reshape(array.shape[1], H * DH)


def per_device(queries, grad_out, mem_keys, mem_values, block_lists, block_home):
    z = lax.axis_index("dp")
    m = lax.axis_index("mem")
    c, k = m // 2, m % 2
    place = jnp.stack([z, c, k]).astype(jnp.int32)

    q_own, g_own, kv_cat = prepare(place, queries, grad_out, mem_keys, mem_values)
    lists = tuple(over_z(block_lists, shift) for shift in (-1, 2, 1))
    kv_cat, lists = lax.optimization_barrier((kv_cat, lists))
    ents = make_list(place, (block_lists,) + lists, block_home)
    q_prev = over_z(q_own, 1)
    g_next = over_z(g_own, -1)
    g_prev = over_z(g_own, 1)
    q_next = over_z(q_own, -1)
    kv_own, q_prev, g_next, g_prev, q_next, ents = lax.optimization_barrier(
        (plane_exchange(kv_cat), q_prev, g_next, g_prev, q_next, ents)
    )
    q_far = over_z(q_prev, 1)
    g_far = over_z(g_next, -1)
    kvs = (kv_own, swap_cores(kv_own))
    xparts = (q_own, q_next, q_far, q_prev, g_own, g_next, g_far, g_prev)

    stat = jnp.zeros((3, NQ, DH), F32)
    stat = forward(EARLY, 0, ents, stat, (q_own, q_next, q_prev), (g_own, g_next, g_prev), kvs)
    stat = forward(LATE, LATE_AT, ents, stat, (q_far,), (g_far,), kvs)
    stats = (stat, over_z(stat, 1), over_z(stat, 2), over_z(stat, -1))
    dq0, dq1, dq2, dq3, own, other = backward(ents, stats, xparts, kvs)

    both = (own + swap_cores(other).astype(F32)).astype(BF)
    got = plane_exchange(both)
    k_own, v_own = rows_first(got[:, :BLK]), rows_first(got[:, BLK:])
    v_prev = over_z(v_own, 1)
    v_next = over_z(v_own, -1)
    k_next = over_z(k_own, -1)
    k_prev = over_z(k_own, 1)
    dq_sum = (
        dq0
        + over_z(dq1, 1).astype(F32)
        + over_z(dq3, -1).astype(F32)
        + over_z(dq2, 2).astype(F32)
    ).astype(BF)
    half = BLK // 2
    keep = lax.dynamic_slice_in_dim(dq_sum, k * half, half, 1)
    give = lax.dynamic_slice_in_dim(dq_sum, (1 - k) * half, half, 1)
    got = swap_cores(give)
    whole = jnp.where(
        k == 0, jnp.concatenate([keep, got], axis=0), jnp.concatenate([got, keep], axis=0)
    )
    whole, v_prev, k_next = lax.optimization_barrier((whole, v_prev, k_next))
    v_far = over_z(v_prev, 1)
    k_far = over_z(k_next, -1)
    near = place_near(place, (k_own, k_next, k_prev), (v_own, v_next, v_prev))
    grad_keys, grad_values = place_far(place, near, k_far, v_far)
    grad_queries = rows_first(plane_exchange(whole))
    return grad_queries, grad_keys, grad_values


def solution(mesh):
    in_specs = (P("dp", None), P("dp", None), P("mem", None), P("mem", None), P("dp", None), P())
    out_specs = (P(("dp", "mem"), None), P("mem", None), P("mem", None))
    return jax.shard_map(
        per_device, mesh=mesh, in_specs=in_specs, out_specs=out_specs, check_vma=False
    )
```

```python
import functools

import jax
import jax.numpy as jnp
from jax import lax
from jax.experimental import pallas as pl
from jax.experimental.pallas import tpu as pltpu
from jax.sharding import PartitionSpec as P

H = 16
DH = 128
BLK = 128
TOPB = 16
NZ = 4
NCHIP = 16
QPER = 8
NQ = NZ * QPER
NB = 2 * NCHIP
NENT = NQ * TOPB
EARLY = (0, 1, 3)
LATE = (2,)
LATE_AT = len(EARLY) * QPER * TOPB + 8
COUNT = LATE_AT + len(LATE) * QPER * TOPB + 8
NCOPY = 2 * NZ + 2
CHUNKS = 4
UNROLL_F = 8
UNROLL_B = 8
SCALE = DH ** (-0.5)
BF = jnp.bfloat16
F32 = jnp.float32
MB = 1 << 20


NT = (((1,), (1,)), ((), ()))
NN = (((1,), (0,)), ((), ()))
TN = (((0,), (0,)), ((), ()))


def position():
    m = lax.axis_index("mem")
    return lax.axis_index("dp"), m >> 1, m & 1


def dot(a, b, dims):
    return lax.dot_general(a, b, dims, preferred_element_type=F32)


def over_z(array, shift):
    return lax.ppermute(array, "dp", [(i, (i + shift) % NZ) for i in range(NZ)])


def swap_cores(array):
    return lax.ppermute(array, "mem", [(i, i ^ 1) for i in range(2 * NCHIP)])


def plane_exchange(array):
    groups = [[2 * c + k for c in range(NCHIP)] for k in range(2)]
    return lax.all_to_all(array, "mem", 0, 0, axis_index_groups=groups)


def prepare_kernel(queries, grads, keys, values, q, g, kv, sems):
    z, c, k = position()
    cols = pl.ds(pl.multiple_of(c * DH, DH), DH)
    pairs = []
    for i in range(QPER):
        rows = pl.ds(pl.multiple_of((k * QPER + i) * BLK, BLK), BLK)
        pairs.append((queries.at[rows, cols], q.at[i]))
        pairs.append((grads.at[rows, cols], g.at[i]))
    rows = pl.ds(pl.multiple_of(z * BLK, BLK), BLK)
    for h in range(H):
        cols = slice(h * DH, (h + 1) * DH)
        pairs.append((keys.at[rows, cols], kv.at[h, :BLK]))
        pairs.append((values.at[rows, cols], kv.at[h, BLK:]))
    copies = [pltpu.make_async_copy(a, b, sems.at[n]) for n, (a, b) in enumerate(pairs)]
    for copy in copies:
        copy.start()
    for copy in copies:
        copy.wait()


def prepare(queries, grads, keys, values):
    vmem = pl.BlockSpec(memory_space=pltpu.VMEM)
    far = pl.BlockSpec(memory_space=pl.ANY)
    return pl.pallas_call(
        prepare_kernel,
        out_shape=(
            jax.ShapeDtypeStruct((QPER, BLK, DH), BF),
            jax.ShapeDtypeStruct((QPER, BLK, DH), BF),
            jax.ShapeDtypeStruct((H, 2 * BLK, DH), BF),
        ),
        in_specs=[far] * 4,
        out_specs=(vmem, vmem, vmem),
        scratch_shapes=[pltpu.SemaphoreType.DMA((2 * QPER + 2 * H,))],
        compiler_params=pltpu.CompilerParams(vmem_limit_bytes=60 * MB),
        name="prepare",
    )(queries, grads, keys, values)


def list_kernel(l0, l1, l2, l3, home, ents):
    z, _, k = position()

    def group(r, lists, n):
        def block(i, n):
            q = r * QPER + i
            seen = jnp.int32(0)
            for t in range(TOPB):
                slot = home[lists[k * QPER + i, t]]
                mine = (slot & 3) == z
                owner = slot >> 2
                b = ((owner & 1) ^ k) * NCHIP + (owner >> 1)
                ents[n] = (q << 15) | ((seen * NQ + q) << 5) | b
                step = mine.astype(jnp.int32)
                n = n + step
                seen = seen + step
            return n

        return lax.fori_loop(0, QPER, block, n)

    every = (l0, l1, l2, l3)
    for part, (start, groups) in enumerate(((0, EARLY), (LATE_AT, LATE))):
        n = jnp.int32(start)
        for r in groups:
            n = group(r, every[r], n)
        for u in range(8):
            ents[n + u] = ((NQ + groups[0] * QPER) << 15) | (NENT << 5)
        ents[COUNT + part] = n - start


def make_list(lists, home):
    smem = pl.BlockSpec(memory_space=pltpu.SMEM)
    return pl.pallas_call(
        list_kernel,
        out_shape=jax.ShapeDtypeStruct((COUNT + 8,), jnp.int32),
        in_specs=[smem] * 5,
        out_specs=smem,
        compiler_params=pltpu.CompilerParams(vmem_limit_bytes=MB),
        name="entry_list",
    )(*lists, home)


def fetch(groups, qrefs, grefs, kvrefs, qs, gs, kv, sems):
    pairs = [(ref, kv.at[p]) for p, ref in enumerate(kvrefs)]
    pairs += [(ref, qs.at[r]) for r, ref in zip(groups, qrefs)]
    pairs += [(ref, gs.at[r]) for r, ref in zip(groups, grefs)]
    copies = [pltpu.make_async_copy(a, b, sems.at[n]) for n, (a, b) in enumerate(pairs)]
    for copy in copies:
        copy.start()
    return copies


def unpack(p):
    q = p >> 15
    b = p & 31
    return (q >> 3) & 3, q & 7, q, (p >> 5) & 1023, b >> 4, b & 15


def fwd_kernel(groups, start, ents, before, *refs):
    size = len(groups)
    out, qs, gs, kv, st, sems = refs[2 * size + 2 :]
    copies = fetch(
        groups, refs[:size], refs[size : 2 * size], refs[2 * size : 2 * size + 2], qs, gs, kv, sems
    )
    st[0] = jnp.full((NENT + 8, DH), -1e30, F32)
    st[1] = jnp.zeros((NENT + 8, DH), F32)
    st[2] = jnp.zeros((NENT + 8, DH), F32)
    for copy in copies:
        copy.wait()

    def body(n, carry):
        parts = [unpack(ents[start + UNROLL_F * n + u]) for u in range(UNROLL_F)]
        scores = [dot(kv[p[4], p[5], :BLK], qs[p[0], p[1]], NT) * SCALE for p in parts]
        dprob = [dot(kv[p[4], p[5], BLK:], gs[p[0], p[1]], NT) for p in parts]
        highs = [jnp.max(x, axis=0, keepdims=True) for x in scores]
        expo = [jnp.exp(x - high) for x, high in zip(scores, highs)]
        for p, high, e, d in zip(parts, highs, expo, dprob):
            row = pl.ds(p[3], 1)
            st[0, row, :] = high
            st[1, row, :] = jnp.sum(e, axis=0, keepdims=True)
            st[2, row, :] = jnp.sum(e.astype(BF).astype(F32) * d, axis=0, keepdims=True)
        return carry

    part = 0 if start == 0 else 1
    lax.fori_loop(0, (ents[COUNT + part] + UNROLL_F - 1) // UNROLL_F, body, 0)
    out[...] = before[...]
    for r in groups:
        rows = [slice(e * NQ + r * QPER, e * NQ + (r + 1) * QPER) for e in range(TOPB)]
        high = st[0, rows[0]]
        for row in rows[1:]:
            high = jnp.maximum(high, st[0, row])
        total = jnp.zeros((QPER, DH), F32)
        prod = jnp.zeros((QPER, DH), F32)
        for row in rows:
            weight = jnp.exp(st[0, row] - high)
            total = total + weight * st[1, row]
            prod = prod + weight * st[2, row]
        at = slice(r * QPER, (r + 1) * QPER)
        out[0, at] = high
        out[1, at] = total
        out[2, at] = prod


def scratch_in():
    return [
        pltpu.VMEM((NZ, QPER, BLK, DH), BF),
        pltpu.VMEM((NZ, QPER, BLK, DH), BF),
        pltpu.VMEM((2, NCHIP, 2 * BLK, DH), BF),
    ]


def forward(groups, start, ents, before, qparts, gparts, kvs):
    smem = pl.BlockSpec(memory_space=pltpu.SMEM)
    vmem = pl.BlockSpec(memory_space=pltpu.VMEM)
    far = pl.BlockSpec(memory_space=pl.ANY)
    return pl.pallas_call(
        functools.partial(fwd_kernel, groups, start),
        out_shape=jax.ShapeDtypeStruct((3, NQ, DH), F32),
        in_specs=[smem, vmem] + [far] * (2 * len(groups) + 2),
        out_specs=vmem,
        scratch_shapes=scratch_in()
        + [pltpu.VMEM((3, NENT + 8, DH), F32), pltpu.SemaphoreType.DMA((NCOPY,))],
        compiler_params=pltpu.CompilerParams(vmem_limit_bytes=14 * MB),
        name="forward",
    )(ents, before, *qparts, *gparts, *kvs)


def bwd_kernel(
    ents, s0, s1, s2, s3, q0, q1, q2, q3, g0, g1, g2, g3, kva, kvb,
    dq0, dq1, dq2, dq3, own, other,
    qs, gs, kv, dq, dkv, away, dqs, lse, delta, sems, outsems,
):
    copies = fetch(range(NZ), (q0, q1, q2, q3), (g0, g1, g2, g3), (kva, kvb), qs, gs, kv, sems)

    def clear(i, carry):
        zero = jnp.zeros((BLK, DH), F32)
        dq[i] = zero
        dkv[i, :BLK] = zero
        dkv[i, BLK:] = zero
        return carry

    lax.fori_loop(0, NQ, clear, 0)
    for r in range(NZ):
        rows = slice(r * QPER, (r + 1) * QPER)
        parts = []
        for ref, shift in ((s0, 0), (s1, 1), (s2, 2), (s3, 3)):
            at = (r + shift) % NZ
            parts.append([ref[n, at * QPER : (at + 1) * QPER] for n in range(3)])
        high = jnp.maximum(
            jnp.maximum(parts[0][0], parts[1][0]), jnp.maximum(parts[2][0], parts[3][0])
        )
        total = jnp.zeros((QPER, DH), F32)
        prod = jnp.zeros((QPER, DH), F32)
        for part in parts:
            weight = jnp.exp(part[0] - high)
            total = total + weight * part[1]
            prod = prod + weight * part[2]
        lse[rows] = high + jnp.log(total)
        delta[rows] = prod / total
    for copy in copies:
        copy.wait()

    lse[NQ:] = jnp.full((NQ, DH), 1e30, F32)
    delta[NQ:] = jnp.zeros((NQ, DH), F32)

    early = (ents[COUNT] + UNROLL_B - 1) // UNROLL_B
    late = (ents[COUNT + 1] + UNROLL_B - 1) // UNROLL_B

    def body(n, carry):
        at = jnp.where(n < early, n * UNROLL_B, LATE_AT + (n - early) * UNROLL_B)
        parts = [unpack(ents[at + u]) for u in range(UNROLL_B)]
        keys = [kv[p[4], p[5], :BLK] for p in parts]
        quer = [qs[p[0], p[1]] for p in parts]
        grad = [gs[p[0], p[1]] for p in parts]
        scores = [dot(a, b, NT) * SCALE for a, b in zip(keys, quer)]
        dprob = [dot(kv[p[4], p[5], BLK:], b, NT) for p, b in zip(parts, grad)]
        probs = [jnp.exp(x - lse[pl.ds(p[2], 1), :]) for x, p in zip(scores, parts)]
        dscore = [
            (x * (d - delta[pl.ds(p[2], 1), :]) * SCALE).astype(BF)
            for x, d, p in zip(probs, dprob, parts)
        ]
        gv = [dot(x.astype(BF), b, NN) for x, b in zip(probs, grad)]
        gk = [dot(x, b, NN) for x, b in zip(dscore, quer)]
        gq = [dot(x, b, TN) for x, b in zip(dscore, keys)]
        for p, a, b, c in zip(parts, gv, gk, gq):
            at = p[4] * NCHIP + p[5]
            dkv[at, BLK:] += a
            dkv[at, :BLK] += b
            dq[p[0] * QPER + p[1]] += c
        return carry

    lax.fori_loop(0, early + late, body, 0)
    sends = []
    for n, ref in ((1, other), (0, own)):
        half = slice(n * NCHIP, (n + 1) * NCHIP)
        away[half] = dkv[half].astype(BF)
        sends.append(pltpu.make_async_copy(away.at[half], ref, outsems.at[n]))
        sends[-1].start()
    for r, ref in enumerate((dq0, dq1, dq2, dq3)):
        part = slice(r * QPER, (r + 1) * QPER)
        dqs[part] = dq[part].astype(BF)
        sends.append(pltpu.make_async_copy(dqs.at[part], ref, outsems.at[2 + r]))
        sends[-1].start()
    for send in sends:
        send.wait()


def backward(ents, stats, xparts, kvs):
    smem = pl.BlockSpec(memory_space=pltpu.SMEM)
    vmem = pl.BlockSpec(memory_space=pltpu.VMEM)
    far = pl.BlockSpec(memory_space=pl.ANY)
    tile = (BLK, DH)
    outs = [jax.ShapeDtypeStruct((QPER,) + tile, BF)] * 4
    pair = (NCHIP, 2 * BLK, DH)
    outs += [jax.ShapeDtypeStruct(pair, BF)] * 2
    return pl.pallas_call(
        bwd_kernel,
        out_shape=tuple(outs),
        in_specs=[smem] + [vmem] * 4 + [far] * 10,
        out_specs=tuple([far] * 6),
        scratch_shapes=scratch_in()
        + [
            pltpu.VMEM((NQ,) + tile, F32),
            pltpu.VMEM((NB, 2 * BLK, DH), F32),
            pltpu.VMEM((NB, 2 * BLK, DH), BF),
            pltpu.VMEM((NQ,) + tile, BF),
            pltpu.VMEM((2 * NQ, DH), F32),
            pltpu.VMEM((2 * NQ, DH), F32),
            pltpu.SemaphoreType.DMA((NCOPY,)),
            pltpu.SemaphoreType.DMA((6,)),
        ],
        compiler_params=pltpu.CompilerParams(vmem_limit_bytes=24 * MB),
        name="backward",
    )(ents, *stats, *xparts, *kvs)


def place_parts(z, parts, sems):
    copies = []
    for n, (r, ref, out) in enumerate(parts):
        rows = pl.ds(pl.multiple_of(((z + r) & 3) * BLK, BLK), BLK)
        copies.append(pltpu.make_async_copy(ref, out.at[rows], sems.at[n]))
    for copy in copies:
        copy.start()
    for copy in copies:
        copy.wait()


def near_kernel(k0, k1, k3, v0, v1, v3, outk, outv, sems):
    parts = [(0, k0, outk), (1, k1, outk), (3, k3, outk)]
    parts += [(0, v0, outv), (1, v1, outv), (3, v3, outv)]
    place_parts(position()[0], parts, sems)


def far_kernel(k2, v2, ink, inv, outk, outv, held, insems, outsems):
    z = position()[0]
    rows = BLK // CHUNKS
    came, went = [], []
    for n in range(CHUNKS):
        for t, (ref, out) in enumerate(((k2, outk), (v2, outv))):
            at = pl.ds(n * rows, rows)
            to = pl.ds(pl.multiple_of(((z + 2) & 3) * BLK + n * rows, rows), rows)
            s = 2 * n + t
            came.append(pltpu.make_async_copy(ref.at[at], held.at[t, at], insems.at[s]))
            went.append(pltpu.make_async_copy(held.at[t, at], out.at[to], outsems.at[s]))
    for copy in came:
        copy.start()
    for first, second in zip(came, went):
        first.wait()
        second.start()
    for copy in went:
        copy.wait()


def place_near(kparts, vparts):
    smem = pl.BlockSpec(memory_space=pltpu.SMEM)
    vmem = pl.BlockSpec(memory_space=pltpu.VMEM)
    far = pl.BlockSpec(memory_space=pl.ANY)
    shape = jax.ShapeDtypeStruct((NZ * BLK, H * DH), BF)
    return pl.pallas_call(
        near_kernel,
        out_shape=(shape, shape),
        in_specs=[vmem] * 6,
        out_specs=(far, far),
        scratch_shapes=[pltpu.SemaphoreType.DMA((6,))],
        compiler_params=pltpu.CompilerParams(vmem_limit_bytes=8 * MB),
        name="place_near",
    )(*kparts, *vparts)


def place_far(near, k_far, v_far):
    far = pl.BlockSpec(memory_space=pl.ANY)
    shape = jax.ShapeDtypeStruct((NZ * BLK, H * DH), BF)
    return pl.pallas_call(
        far_kernel,
        out_shape=(shape, shape),
        in_specs=[far] * 4,
        out_specs=(far, far),
        scratch_shapes=[
            pltpu.VMEM((2, BLK, H * DH), BF),
            pltpu.SemaphoreType.DMA((2 * CHUNKS,)),
            pltpu.SemaphoreType.DMA((2 * CHUNKS,)),
        ],
        input_output_aliases={2: 0, 3: 1},
        compiler_params=pltpu.CompilerParams(vmem_limit_bytes=8 * MB),
        name="place_far",
    )(k_far, v_far, *near)


def heads_first(array):
    return jnp.transpose(array.reshape(array.shape[0], H, DH), (1, 0, 2))


def rows_first(array):
    return jnp.transpose(array, (1, 0, 2)).reshape(array.shape[1], H * DH)


def per_device(queries, grad_out, mem_keys, mem_values, block_lists, block_home):
    k = lax.axis_index("mem") & 1
    q_own, g_own, kv_cat = prepare(queries, grad_out, mem_keys, mem_values)
    lists = tuple(over_z(block_lists, shift) for shift in (-1, 2, 1))
    kv_cat, lists = lax.optimization_barrier((kv_cat, lists))
    ents = make_list((block_lists,) + lists, block_home)
    q_prev = over_z(q_own, 1)
    g_next = over_z(g_own, -1)
    g_prev = over_z(g_own, 1)
    q_next = over_z(q_own, -1)
    kv_own, q_prev, g_next, g_prev, q_next, ents = lax.optimization_barrier(
        (plane_exchange(kv_cat), q_prev, g_next, g_prev, q_next, ents)
    )
    q_far = over_z(q_prev, 1)
    g_far = over_z(g_next, -1)
    kvs = (kv_own, swap_cores(kv_own))
    xparts = (q_own, q_next, q_far, q_prev, g_own, g_next, g_far, g_prev)

    stat = jnp.zeros((3, NQ, DH), F32)
    stat = forward(EARLY, 0, ents, stat, (q_own, q_next, q_prev), (g_own, g_next, g_prev), kvs)
    stat = forward(LATE, LATE_AT, ents, stat, (q_far,), (g_far,), kvs)
    stats = (stat, over_z(stat, 1), over_z(stat, 2), over_z(stat, -1))
    dq0, dq1, dq2, dq3, own, other = backward(ents, stats, xparts, kvs)

    both = (own.astype(F32) + swap_cores(other).astype(F32)).astype(BF)
    got = plane_exchange(both)
    k_own, v_own = rows_first(got[:, :BLK]), rows_first(got[:, BLK:])
    v_prev = over_z(v_own, 1)
    v_next = over_z(v_own, -1)
    k_next = over_z(k_own, -1)
    k_prev = over_z(k_own, 1)
    dq_sum = (
        dq0.astype(F32)
        + over_z(dq1, 1).astype(F32)
        + over_z(dq3, -1).astype(F32)
        + over_z(dq2, 2).astype(F32)
    ).astype(BF)
    half = BLK // 2
    keep = lax.dynamic_slice_in_dim(dq_sum, k * half, half, 1)
    give = lax.dynamic_slice_in_dim(dq_sum, (1 - k) * half, half, 1)
    got = swap_cores(give)
    whole = jnp.where(
        k == 0, jnp.concatenate([keep, got], axis=0), jnp.concatenate([got, keep], axis=0)
    )
    whole, v_prev, k_next = lax.optimization_barrier((whole, v_prev, k_next))
    v_far = over_z(v_prev, 1)
    k_far = over_z(k_next, -1)
    near = place_near((k_own, k_next, k_prev), (v_own, v_next, v_prev))
    grad_keys, grad_values = place_far(near, k_far, v_far)
    grad_queries = rows_first(plane_exchange(whole))
    return grad_queries, grad_keys, grad_values


def solution(mesh):
    in_specs = (P("dp", None), P("dp", None), P("mem", None), P("mem", None), P("dp", None), P())
    out_specs = (P(("dp", "mem"), None), P("mem", None), P("mem", None))
    return jax.shard_map(
        per_device, mesh=mesh, in_specs=in_specs, out_specs=out_specs, check_vma=False
    )
```

```python
import functools

import jax
import jax.numpy as jnp
from jax import lax
from jax.experimental import pallas as pl
from jax.experimental.pallas import tpu as pltpu
from jax.sharding import PartitionSpec as P

H = 16
DH = 128
BLK = 128
TOPB = 16
NZ = 4
NCHIP = 16
QPER = 8
NQ = NZ * QPER
NB = 2 * NCHIP
NENT = NQ * TOPB
EARLY = (0, 1, 3)
LATE = (2,)
LATE_AT = len(EARLY) * QPER * TOPB + 8
COUNT = LATE_AT + len(LATE) * QPER * TOPB + 16
NCOPY = 2 * NZ + 2
CHUNKS = 4
UNROLL_F = 8
UNROLL_B = 16
SCALE = DH ** (-0.5)
BF = jnp.bfloat16
F32 = jnp.float32
MB = 1 << 20


NT = (((1,), (1,)), ((), ()))
NN = (((1,), (0,)), ((), ()))
TN = (((0,), (0,)), ((), ()))


def position():
    m = lax.axis_index("mem")
    return lax.axis_index("dp"), m >> 1, m & 1


def dot(a, b, dims):
    return lax.dot_general(a, b, dims, preferred_element_type=F32)


def over_z(array, shift):
    return lax.ppermute(array, "dp", [(i, (i + shift) % NZ) for i in range(NZ)])


def swap_cores(array):
    return lax.ppermute(array, "mem", [(i, i ^ 1) for i in range(2 * NCHIP)])


def plane_exchange(array):
    groups = [[2 * c + k for c in range(NCHIP)] for k in range(2)]
    return lax.all_to_all(array, "mem", 0, 0, axis_index_groups=groups)


def prepare_kernel(queries, grads, keys, values, q, g, kv, sems):
    z, c, k = position()
    cols = pl.ds(pl.multiple_of(c * DH, DH), DH)
    pairs = []
    for i in range(QPER):
        rows = pl.ds(pl.multiple_of((k * QPER + i) * BLK, BLK), BLK)
        pairs.append((queries.at[rows, cols], q.at[i]))
        pairs.append((grads.at[rows, cols], g.at[i]))
    rows = pl.ds(pl.multiple_of(z * BLK, BLK), BLK)
    for h in range(H):
        cols = slice(h * DH, (h + 1) * DH)
        pairs.append((keys.at[rows, cols], kv.at[h, :BLK]))
        pairs.append((values.at[rows, cols], kv.at[h, BLK:]))
    copies = [pltpu.make_async_copy(a, b, sems.at[n]) for n, (a, b) in enumerate(pairs)]
    for copy in copies:
        copy.start()
    for copy in copies:
        copy.wait()


def prepare(queries, grads, keys, values):
    vmem = pl.BlockSpec(memory_space=pltpu.VMEM)
    far = pl.BlockSpec(memory_space=pl.ANY)
    return pl.pallas_call(
        prepare_kernel,
        out_shape=(
            jax.ShapeDtypeStruct((QPER, BLK, DH), BF),
            jax.ShapeDtypeStruct((QPER, BLK, DH), BF),
            jax.ShapeDtypeStruct((H, 2 * BLK, DH), BF),
        ),
        in_specs=[far] * 4,
        out_specs=(vmem, vmem, vmem),
        scratch_shapes=[pltpu.SemaphoreType.DMA((2 * QPER + 2 * H,))],
        compiler_params=pltpu.CompilerParams(vmem_limit_bytes=60 * MB),
        name="prepare",
    )(queries, grads, keys, values)


def list_kernel(l0, l1, l2, l3, home, ents):
    z, _, k = position()

    def group(r, lists, n):
        def block(i, n):
            q = r * QPER + i
            seen = jnp.int32(0)
            for t in range(TOPB):
                slot = home[lists[k * QPER + i, t]]
                mine = (slot & 3) == z
                owner = slot >> 2
                b = ((owner & 1) ^ k) * NCHIP + (owner >> 1)
                ents[n] = (q << 15) | ((seen * NQ + q) << 5) | b
                step = mine.astype(jnp.int32)
                n = n + step
                seen = seen + step
            return n

        return lax.fori_loop(0, QPER, block, n)

    every = (l0, l1, l2, l3)
    for part, (start, groups) in enumerate(((0, EARLY), (LATE_AT, LATE))):
        n = jnp.int32(start)
        for r in groups:
            n = group(r, every[r], n)
        for u in range(8 if start == 0 else 16):
            ents[n + u] = ((NQ + groups[0] * QPER) << 15) | (NENT << 5)
        ents[COUNT + part] = n - start


def make_list(lists, home):
    smem = pl.BlockSpec(memory_space=pltpu.SMEM)
    return pl.pallas_call(
        list_kernel,
        out_shape=jax.ShapeDtypeStruct((COUNT + 8,), jnp.int32),
        in_specs=[smem] * 5,
        out_specs=smem,
        compiler_params=pltpu.CompilerParams(vmem_limit_bytes=MB),
        name="entry_list",
    )(*lists, home)


def fetch(groups, qrefs, grefs, kvrefs, qs, gs, kv, sems):
    pairs = [(ref, kv.at[p]) for p, ref in enumerate(kvrefs)]
    pairs += [(ref, qs.at[r]) for r, ref in zip(groups, qrefs)]
    pairs += [(ref, gs.at[r]) for r, ref in zip(groups, grefs)]
    copies = [pltpu.make_async_copy(a, b, sems.at[n]) for n, (a, b) in enumerate(pairs)]
    for copy in copies:
        copy.start()
    return copies


def unpack(p):
    q = p >> 15
    b = p & 31
    return (q >> 3) & 3, q & 7, q, (p >> 5) & 1023, b >> 4, b & 15


def fwd_kernel(groups, start, ents, before, *refs):
    size = len(groups)
    out, qs, gs, kv, st, sems = refs[2 * size + 2 :]
    copies = fetch(
        groups, refs[:size], refs[size : 2 * size], refs[2 * size : 2 * size + 2], qs, gs, kv, sems
    )
    st[0] = jnp.full((NENT + 8, DH), -1e30, F32)
    st[1] = jnp.zeros((NENT + 8, DH), F32)
    st[2] = jnp.zeros((NENT + 8, DH), F32)
    for copy in copies:
        copy.wait()

    def body(n, carry):
        parts = [unpack(ents[start + UNROLL_F * n + u]) for u in range(UNROLL_F)]
        scores = [dot(kv[p[4], p[5], :BLK], qs[p[0], p[1]], NT) * SCALE for p in parts]
        dprob = [dot(kv[p[4], p[5], BLK:], gs[p[0], p[1]], NT) for p in parts]
        highs = [jnp.max(x, axis=0, keepdims=True) for x in scores]
        expo = [jnp.exp(x - high) for x, high in zip(scores, highs)]
        for p, high, e, d in zip(parts, highs, expo, dprob):
            row = pl.ds(p[3], 1)
            st[0, row, :] = high
            st[1, row, :] = jnp.sum(e, axis=0, keepdims=True)
            st[2, row, :] = jnp.sum(e.astype(BF).astype(F32) * d, axis=0, keepdims=True)
        return carry

    part = 0 if start == 0 else 1
    lax.fori_loop(0, (ents[COUNT + part] + UNROLL_F - 1) // UNROLL_F, body, 0)
    out[...] = before[...]
    for r in groups:
        rows = [slice(e * NQ + r * QPER, e * NQ + (r + 1) * QPER) for e in range(TOPB)]
        high = st[0, rows[0]]
        for row in rows[1:]:
            high = jnp.maximum(high, st[0, row])
        total = jnp.zeros((QPER, DH), F32)
        prod = jnp.zeros((QPER, DH), F32)
        for row in rows:
            weight = jnp.exp(st[0, row] - high)
            total = total + weight * st[1, row]
            prod = prod + weight * st[2, row]
        at = slice(r * QPER, (r + 1) * QPER)
        out[0, at] = high
        out[1, at] = total
        out[2, at] = prod


def scratch_in():
    return [
        pltpu.VMEM((NZ, QPER, BLK, DH), BF),
        pltpu.VMEM((NZ, QPER, BLK, DH), BF),
        pltpu.VMEM((2, NCHIP, 2 * BLK, DH), BF),
    ]


def forward(groups, start, ents, before, qparts, gparts, kvs):
    smem = pl.BlockSpec(memory_space=pltpu.SMEM)
    vmem = pl.BlockSpec(memory_space=pltpu.VMEM)
    far = pl.BlockSpec(memory_space=pl.ANY)
    return pl.pallas_call(
        functools.partial(fwd_kernel, groups, start),
        out_shape=jax.ShapeDtypeStruct((3, NQ, DH), F32),
        in_specs=[smem, vmem] + [far] * (2 * len(groups) + 2),
        out_specs=vmem,
        scratch_shapes=scratch_in()
        + [pltpu.VMEM((3, NENT + 8, DH), F32), pltpu.SemaphoreType.DMA((NCOPY,))],
        compiler_params=pltpu.CompilerParams(vmem_limit_bytes=14 * MB),
        name="forward",
    )(ents, before, *qparts, *gparts, *kvs)


def bwd_kernel(
    ents, s0, s1, s2, s3, q0, q1, q2, q3, g0, g1, g2, g3, kva, kvb,
    dq0, dq1, dq2, dq3, own, other,
    qs, gs, kv, dq, dkv, away, dqs, lse, delta, sems, outsems,
):
    copies = fetch(range(NZ), (q0, q1, q2, q3), (g0, g1, g2, g3), (kva, kvb), qs, gs, kv, sems)

    def clear(i, carry):
        zero = jnp.zeros((BLK, DH), F32)
        dq[i] = zero
        dkv[i, :BLK] = zero
        dkv[i, BLK:] = zero
        return carry

    lax.fori_loop(0, NQ, clear, 0)
    for r in range(NZ):
        rows = slice(r * QPER, (r + 1) * QPER)
        parts = []
        for ref, shift in ((s0, 0), (s1, 1), (s2, 2), (s3, 3)):
            at = (r + shift) % NZ
            parts.append([ref[n, at * QPER : (at + 1) * QPER] for n in range(3)])
        high = jnp.maximum(
            jnp.maximum(parts[0][0], parts[1][0]), jnp.maximum(parts[2][0], parts[3][0])
        )
        total = jnp.zeros((QPER, DH), F32)
        prod = jnp.zeros((QPER, DH), F32)
        for part in parts:
            weight = jnp.exp(part[0] - high)
            total = total + weight * part[1]
            prod = prod + weight * part[2]
        lse[rows] = high + jnp.log(total)
        delta[rows] = prod / total
    for copy in copies:
        copy.wait()

    lse[NQ:] = jnp.full((NQ, DH), 1e30, F32)
    delta[NQ:] = jnp.zeros((NQ, DH), F32)

    early = ents[COUNT]
    steps = (early + ents[COUNT + 1] + UNROLL_B - 1) // UNROLL_B

    def body(n, carry):
        parts = []
        for u in range(UNROLL_B):
            at = n * UNROLL_B + u
            parts.append(unpack(ents[jnp.where(at < early, at, at + (LATE_AT - early))]))
        keys = [kv[p[4], p[5], :BLK] for p in parts]
        quer = [qs[p[0], p[1]] for p in parts]
        grad = [gs[p[0], p[1]] for p in parts]
        scores = [dot(a, b, NT) * SCALE for a, b in zip(keys, quer)]
        dprob = [dot(kv[p[4], p[5], BLK:], b, NT) for p, b in zip(parts, grad)]
        probs = [jnp.exp(x - lse[pl.ds(p[2], 1), :]) for x, p in zip(scores, parts)]
        dscore = [
            (x * (d - delta[pl.ds(p[2], 1), :]) * SCALE).astype(BF)
            for x, d, p in zip(probs, dprob, parts)
        ]
        gv = [dot(x.astype(BF), b, NN) for x, b in zip(probs, grad)]
        gk = [dot(x, b, NN) for x, b in zip(dscore, quer)]
        gq = [dot(x, b, TN) for x, b in zip(dscore, keys)]
        for p, a, b, c in zip(parts, gv, gk, gq):
            at = p[4] * NCHIP + p[5]
            dkv[at, BLK:] += a
            dkv[at, :BLK] += b
            dq[p[0] * QPER + p[1]] += c
        return carry

    lax.fori_loop(0, steps, body, 0)
    sends = []
    for n, ref in ((1, other), (0, own)):
        half = slice(n * NCHIP, (n + 1) * NCHIP)
        away[half] = dkv[half].astype(BF)
        sends.append(pltpu.make_async_copy(away.at[half], ref, outsems.at[n]))
        sends[-1].start()
    for r, ref in enumerate((dq0, dq1, dq2, dq3)):
        part = slice(r * QPER, (r + 1) * QPER)
        dqs[part] = dq[part].astype(BF)
        sends.append(pltpu.make_async_copy(dqs.at[part], ref, outsems.at[2 + r]))
        sends[-1].start()
    for send in sends:
        send.wait()


def backward(ents, stats, xparts, kvs):
    smem = pl.BlockSpec(memory_space=pltpu.SMEM)
    vmem = pl.BlockSpec(memory_space=pltpu.VMEM)
    far = pl.BlockSpec(memory_space=pl.ANY)
    tile = (BLK, DH)
    outs = [jax.ShapeDtypeStruct((QPER,) + tile, BF)] * 4
    pair = (NCHIP, 2 * BLK, DH)
    outs += [jax.ShapeDtypeStruct(pair, BF)] * 2
    return pl.pallas_call(
        bwd_kernel,
        out_shape=tuple(outs),
        in_specs=[smem] + [vmem] * 4 + [far] * 10,
        out_specs=tuple([far] * 6),
        scratch_shapes=scratch_in()
        + [
            pltpu.VMEM((NQ,) + tile, F32),
            pltpu.VMEM((NB, 2 * BLK, DH), F32),
            pltpu.VMEM((NB, 2 * BLK, DH), BF),
            pltpu.VMEM((NQ,) + tile, BF),
            pltpu.VMEM((2 * NQ, DH), F32),
            pltpu.VMEM((2 * NQ, DH), F32),
            pltpu.SemaphoreType.DMA((NCOPY,)),
            pltpu.SemaphoreType.DMA((6,)),
        ],
        compiler_params=pltpu.CompilerParams(vmem_limit_bytes=24 * MB),
        name="backward",
    )(ents, *stats, *xparts, *kvs)


def place_parts(z, parts, sems):
    copies = []
    for n, (r, ref, out) in enumerate(parts):
        rows = pl.ds(pl.multiple_of(((z + r) & 3) * BLK, BLK), BLK)
        copies.append(pltpu.make_async_copy(ref, out.at[rows], sems.at[n]))
    for copy in copies:
        copy.start()
    for copy in copies:
        copy.wait()


def near_kernel(k0, k1, k3, v0, v1, v3, outk, outv, sems):
    parts = [(0, k0, outk), (1, k1, outk), (3, k3, outk)]
    parts += [(0, v0, outv), (1, v1, outv), (3, v3, outv)]
    place_parts(position()[0], parts, sems)


def far_kernel(k2, v2, ink, inv, outk, outv, held, insems, outsems):
    z = position()[0]
    rows = BLK // CHUNKS
    came, went = [], []
    for n in range(CHUNKS):
        for t, (ref, out) in enumerate(((k2, outk), (v2, outv))):
            at = pl.ds(n * rows, rows)
            to = pl.ds(pl.multiple_of(((z + 2) & 3) * BLK + n * rows, rows), rows)
            s = 2 * n + t
            came.append(pltpu.make_async_copy(ref.at[at], held.at[t, at], insems.at[s]))
            went.append(pltpu.make_async_copy(held.at[t, at], out.at[to], outsems.at[s]))
    for copy in came:
        copy.start()
    for first, second in zip(came, went):
        first.wait()
        second.start()
    for copy in went:
        copy.wait()


def place_near(kparts, vparts):
    smem = pl.BlockSpec(memory_space=pltpu.SMEM)
    vmem = pl.BlockSpec(memory_space=pltpu.VMEM)
    far = pl.BlockSpec(memory_space=pl.ANY)
    shape = jax.ShapeDtypeStruct((NZ * BLK, H * DH), BF)
    return pl.pallas_call(
        near_kernel,
        out_shape=(shape, shape),
        in_specs=[vmem] * 6,
        out_specs=(far, far),
        scratch_shapes=[pltpu.SemaphoreType.DMA((6,))],
        compiler_params=pltpu.CompilerParams(vmem_limit_bytes=8 * MB),
        name="place_near",
    )(*kparts, *vparts)


def place_far(near, k_far, v_far):
    far = pl.BlockSpec(memory_space=pl.ANY)
    shape = jax.ShapeDtypeStruct((NZ * BLK, H * DH), BF)
    return pl.pallas_call(
        far_kernel,
        out_shape=(shape, shape),
        in_specs=[far] * 4,
        out_specs=(far, far),
        scratch_shapes=[
            pltpu.VMEM((2, BLK, H * DH), BF),
            pltpu.SemaphoreType.DMA((2 * CHUNKS,)),
            pltpu.SemaphoreType.DMA((2 * CHUNKS,)),
        ],
        input_output_aliases={2: 0, 3: 1},
        compiler_params=pltpu.CompilerParams(vmem_limit_bytes=8 * MB),
        name="place_far",
    )(k_far, v_far, *near)


def heads_first(array):
    return jnp.transpose(array.reshape(array.shape[0], H, DH), (1, 0, 2))


def rows_first(array):
    return jnp.transpose(array, (1, 0, 2)).reshape(array.shape[1], H * DH)


def per_device(queries, grad_out, mem_keys, mem_values, block_lists, block_home):
    k = lax.axis_index("mem") & 1
    q_own, g_own, kv_cat = prepare(queries, grad_out, mem_keys, mem_values)
    lists = tuple(over_z(block_lists, shift) for shift in (-1, 2, 1))
    kv_cat, lists = lax.optimization_barrier((kv_cat, lists))
    ents = make_list((block_lists,) + lists, block_home)
    q_prev = over_z(q_own, 1)
    g_next = over_z(g_own, -1)
    g_prev = over_z(g_own, 1)
    q_next = over_z(q_own, -1)
    kv_own, q_prev, g_next, g_prev, q_next, ents = lax.optimization_barrier(
        (plane_exchange(kv_cat), q_prev, g_next, g_prev, q_next, ents)
    )
    q_far = over_z(q_prev, 1)
    g_far = over_z(g_next, -1)
    kvs = (kv_own, swap_cores(kv_own))
    xparts = (q_own, q_next, q_far, q_prev, g_own, g_next, g_far, g_prev)

    stat = jnp.zeros((3, NQ, DH), F32)
    stat = forward(EARLY, 0, ents, stat, (q_own, q_next, q_prev), (g_own, g_next, g_prev), kvs)
    stat = forward(LATE, LATE_AT, ents, stat, (q_far,), (g_far,), kvs)
    stats = (stat, over_z(stat, 1), over_z(stat, 2), over_z(stat, -1))
    dq0, dq1, dq2, dq3, own, other = backward(ents, stats, xparts, kvs)

    both = (own.astype(F32) + swap_cores(other).astype(F32)).astype(BF)
    got = plane_exchange(both)
    k_own, v_own = rows_first(got[:, :BLK]), rows_first(got[:, BLK:])
    v_prev = over_z(v_own, 1)
    v_next = over_z(v_own, -1)
    k_next = over_z(k_own, -1)
    k_prev = over_z(k_own, 1)
    dq_sum = (
        dq0.astype(F32)
        + over_z(dq1, 1).astype(F32)
        + over_z(dq3, -1).astype(F32)
        + over_z(dq2, 2).astype(F32)
    ).astype(BF)
    half = BLK // 2
    keep = lax.dynamic_slice_in_dim(dq_sum, k * half, half, 1)
    give = lax.dynamic_slice_in_dim(dq_sum, (1 - k) * half, half, 1)
    got = swap_cores(give)
    whole = jnp.where(
        k == 0, jnp.concatenate([keep, got], axis=0), jnp.concatenate([got, keep], axis=0)
    )
    whole, v_prev, k_next = lax.optimization_barrier((whole, v_prev, k_next))
    v_far = over_z(v_prev, 1)
    k_far = over_z(k_next, -1)
    near = place_near((k_own, k_next, k_prev), (v_own, v_next, v_prev))
    grad_keys, grad_values = place_far(near, k_far, v_far)
    grad_queries = rows_first(plane_exchange(whole))
    return grad_queries, grad_keys, grad_values


def solution(mesh):
    in_specs = (P("dp", None), P("dp", None), P("mem", None), P("mem", None), P("dp", None), P())
    out_specs = (P(("dp", "mem"), None), P("mem", None), P("mem", None))
    return jax.shard_map(
        per_device, mesh=mesh, in_specs=in_specs, out_specs=out_specs, check_vma=False
    )
```

```python
import functools

import jax
import jax.numpy as jnp
from jax import lax
from jax.experimental import pallas as pl
from jax.experimental.pallas import tpu as pltpu
from jax.sharding import PartitionSpec as P

H = 16
DH = 128
BLK = 128
TOPB = 16
NZ = 4
NCHIP = 16
QPER = 8
NQ = NZ * QPER
NB = 2 * NCHIP
NENT = NQ * TOPB
EARLY = (0, 1, 3)
LATE = (2,)
LATE_AT = len(EARLY) * QPER * TOPB + 8
COUNT = LATE_AT + len(LATE) * QPER * TOPB + 16
NCOPY = 2 * NZ + 2
CHUNKS = 4
UNROLL_F = 8
UNROLL_B = 16
SCALE = DH ** (-0.5)
BF = jnp.bfloat16
F32 = jnp.float32
MB = 1 << 20


NT = (((1,), (1,)), ((), ()))
NN = (((1,), (0,)), ((), ()))
TN = (((0,), (0,)), ((), ()))


def position():
    m = lax.axis_index("mem")
    return lax.axis_index("dp"), m >> 1, m & 1


def dot(a, b, dims):
    return lax.dot_general(a, b, dims, preferred_element_type=F32)


def over_z(array, shift):
    return lax.ppermute(array, "dp", [(i, (i + shift) % NZ) for i in range(NZ)])


def swap_cores(array):
    return lax.ppermute(array, "mem", [(i, i ^ 1) for i in range(2 * NCHIP)])


def plane_exchange(array):
    groups = [[2 * c + k for c in range(NCHIP)] for k in range(2)]
    return lax.all_to_all(array, "mem", 0, 0, axis_index_groups=groups)


def prepare_kernel(queries, grads, keys, values, q, g, kv, sems):
    z, c, k = position()
    cols = pl.ds(pl.multiple_of(c * DH, DH), DH)
    pairs = []
    for i in range(QPER):
        rows = pl.ds(pl.multiple_of((k * QPER + i) * BLK, BLK), BLK)
        pairs.append((queries.at[rows, cols], q.at[i]))
        pairs.append((grads.at[rows, cols], g.at[i]))
    rows = pl.ds(pl.multiple_of(z * BLK, BLK), BLK)
    for h in range(H):
        cols = slice(h * DH, (h + 1) * DH)
        pairs.append((keys.at[rows, cols], kv.at[h, :BLK]))
        pairs.append((values.at[rows, cols], kv.at[h, BLK:]))
    copies = [pltpu.make_async_copy(a, b, sems.at[n]) for n, (a, b) in enumerate(pairs)]
    for copy in copies:
        copy.start()
    for copy in copies:
        copy.wait()


def prepare(queries, grads, keys, values):
    vmem = pl.BlockSpec(memory_space=pltpu.VMEM)
    far = pl.BlockSpec(memory_space=pl.ANY)
    return pl.pallas_call(
        prepare_kernel,
        out_shape=(
            jax.ShapeDtypeStruct((QPER, BLK, DH), BF),
            jax.ShapeDtypeStruct((QPER, BLK, DH), BF),
            jax.ShapeDtypeStruct((H, 2 * BLK, DH), BF),
        ),
        in_specs=[far] * 4,
        out_specs=(vmem, vmem, vmem),
        scratch_shapes=[pltpu.SemaphoreType.DMA((2 * QPER + 2 * H,))],
        compiler_params=pltpu.CompilerParams(vmem_limit_bytes=60 * MB),
        name="prepare",
    )(queries, grads, keys, values)


def list_kernel(l0, l1, l2, l3, home, ents):
    z, _, k = position()

    def group(r, lists, n):
        def block(i, n):
            q = r * QPER + i
            seen = jnp.int32(0)
            for t in range(TOPB):
                slot = home[lists[k * QPER + i, t]]
                mine = (slot & 3) == z
                owner = slot >> 2
                b = ((owner & 1) ^ k) * NCHIP + (owner >> 1)
                ents[n] = (q << 15) | ((seen * NQ + q) << 5) | b
                step = mine.astype(jnp.int32)
                n = n + step
                seen = seen + step
            return n

        return lax.fori_loop(0, QPER, block, n)

    every = (l0, l1, l2, l3)
    for part, (start, groups) in enumerate(((0, EARLY), (LATE_AT, LATE))):
        n = jnp.int32(start)
        for r in groups:
            n = group(r, every[r], n)
        for u in range(8 if start == 0 else 16):
            ents[n + u] = ((NQ + groups[0] * QPER) << 15) | (NENT << 5)
        ents[COUNT + part] = n - start


def make_list(lists, home):
    smem = pl.BlockSpec(memory_space=pltpu.SMEM)
    return pl.pallas_call(
        list_kernel,
        out_shape=jax.ShapeDtypeStruct((COUNT + 8,), jnp.int32),
        in_specs=[smem] * 5,
        out_specs=smem,
        compiler_params=pltpu.CompilerParams(vmem_limit_bytes=MB),
        name="entry_list",
    )(*lists, home)


def fetch(groups, qrefs, grefs, kvrefs, qs, gs, kv, sems):
    pairs = [(ref, kv.at[p]) for p, ref in enumerate(kvrefs)]
    pairs += [(ref, qs.at[r]) for r, ref in zip(groups, qrefs)]
    pairs += [(ref, gs.at[r]) for r, ref in zip(groups, grefs)]
    copies = [pltpu.make_async_copy(a, b, sems.at[n]) for n, (a, b) in enumerate(pairs)]
    for copy in copies:
        copy.start()
    return copies


def unpack(p):
    q = p >> 15
    b = p & 31
    return (q >> 3) & 3, q & 7, q, (p >> 5) & 1023, b >> 4, b & 15


def fwd_kernel(groups, start, ents, before, *refs):
    size = len(groups)
    out, qs, gs, kv, st, sems = refs[2 * size + 2 :]
    copies = fetch(
        groups, refs[:size], refs[size : 2 * size], refs[2 * size : 2 * size + 2], qs, gs, kv, sems
    )
    st[0] = jnp.full((NENT + 8, DH), -1e30, F32)
    st[1] = jnp.zeros((NENT + 8, DH), F32)
    st[2] = jnp.zeros((NENT + 8, DH), F32)
    for copy in copies:
        copy.wait()

    def body(n, carry):
        parts = [unpack(ents[start + UNROLL_F * n + u]) for u in range(UNROLL_F)]
        scores = [dot(kv[p[4], p[5], :BLK], qs[p[0], p[1]], NT) * SCALE for p in parts]
        dprob = [dot(kv[p[4], p[5], BLK:], gs[p[0], p[1]], NT) for p in parts]
        highs = [jnp.max(x, axis=0, keepdims=True) for x in scores]
        expo = [jnp.exp(x - high) for x, high in zip(scores, highs)]
        for p, high, e, d in zip(parts, highs, expo, dprob):
            row = pl.ds(p[3], 1)
            st[0, row, :] = high
            st[1, row, :] = jnp.sum(e, axis=0, keepdims=True)
            st[2, row, :] = jnp.sum(e.astype(BF).astype(F32) * d, axis=0, keepdims=True)
        return carry

    part = 0 if start == 0 else 1
    lax.fori_loop(0, (ents[COUNT + part] + UNROLL_F - 1) // UNROLL_F, body, 0)
    out[...] = before[...]
    for r in groups:
        rows = [slice(e * NQ + r * QPER, e * NQ + (r + 1) * QPER) for e in range(TOPB)]
        high = st[0, rows[0]]
        for row in rows[1:]:
            high = jnp.maximum(high, st[0, row])
        total = jnp.zeros((QPER, DH), F32)
        prod = jnp.zeros((QPER, DH), F32)
        for row in rows:
            weight = jnp.exp(st[0, row] - high)
            total = total + weight * st[1, row]
            prod = prod + weight * st[2, row]
        at = slice(r * QPER, (r + 1) * QPER)
        out[0, at] = high
        out[1, at] = total
        out[2, at] = prod


def scratch_in():
    return [
        pltpu.VMEM((NZ, QPER, BLK, DH), BF),
        pltpu.VMEM((NZ, QPER, BLK, DH), BF),
        pltpu.VMEM((2, NCHIP, 2 * BLK, DH), BF),
    ]


def forward(groups, start, ents, before, qparts, gparts, kvs):
    smem = pl.BlockSpec(memory_space=pltpu.SMEM)
    vmem = pl.BlockSpec(memory_space=pltpu.VMEM)
    far = pl.BlockSpec(memory_space=pl.ANY)
    return pl.pallas_call(
        functools.partial(fwd_kernel, groups, start),
        out_shape=jax.ShapeDtypeStruct((3, NQ, DH), F32),
        in_specs=[smem, vmem] + [far] * (2 * len(groups) + 2),
        out_specs=vmem,
        scratch_shapes=scratch_in()
        + [pltpu.VMEM((3, NENT + 8, DH), F32), pltpu.SemaphoreType.DMA((NCOPY,))],
        compiler_params=pltpu.CompilerParams(vmem_limit_bytes=14 * MB),
        name="forward",
    )(ents, before, *qparts, *gparts, *kvs)


def bwd_kernel(
    ents, s0, s1, s2, s3, q0, q1, q2, q3, g0, g1, g2, g3, kva, kvb,
    dq0, dq1, dq2, dq3, own, other,
    qs, gs, kv, dq, dkv, dqs, lse, delta, sems, outsems,
):
    copies = fetch(range(NZ), (q0, q1, q2, q3), (g0, g1, g2, g3), (kva, kvb), qs, gs, kv, sems)

    def clear(i, carry):
        zero = jnp.zeros((BLK, DH), F32)
        dq[i] = zero
        dkv[i, :BLK] = zero
        dkv[i, BLK:] = zero
        return carry

    lax.fori_loop(0, NQ, clear, 0)
    for r in range(NZ):
        rows = slice(r * QPER, (r + 1) * QPER)
        parts = []
        for ref, shift in ((s0, 0), (s1, 1), (s2, 2), (s3, 3)):
            at = (r + shift) % NZ
            parts.append([ref[n, at * QPER : (at + 1) * QPER] for n in range(3)])
        high = jnp.maximum(
            jnp.maximum(parts[0][0], parts[1][0]), jnp.maximum(parts[2][0], parts[3][0])
        )
        total = jnp.zeros((QPER, DH), F32)
        prod = jnp.zeros((QPER, DH), F32)
        for part in parts:
            weight = jnp.exp(part[0] - high)
            total = total + weight * part[1]
            prod = prod + weight * part[2]
        lse[rows] = high + jnp.log(total)
        delta[rows] = prod / total
    for copy in copies:
        copy.wait()

    lse[NQ:] = jnp.full((NQ, DH), 1e30, F32)
    delta[NQ:] = jnp.zeros((NQ, DH), F32)

    early = ents[COUNT]
    steps = (early + ents[COUNT + 1] + UNROLL_B - 1) // UNROLL_B

    def body(n, carry):
        parts = []
        for u in range(UNROLL_B):
            at = n * UNROLL_B + u
            parts.append(unpack(ents[jnp.where(at < early, at, at + (LATE_AT - early))]))
        keys = [kv[p[4], p[5], :BLK] for p in parts]
        quer = [qs[p[0], p[1]] for p in parts]
        grad = [gs[p[0], p[1]] for p in parts]
        scores = [dot(a, b, NT) * SCALE for a, b in zip(keys, quer)]
        dprob = [dot(kv[p[4], p[5], BLK:], b, NT) for p, b in zip(parts, grad)]
        probs = [jnp.exp(x - lse[pl.ds(p[2], 1), :]) for x, p in zip(scores, parts)]
        dscore = [
            (x * (d - delta[pl.ds(p[2], 1), :]) * SCALE).astype(BF)
            for x, d, p in zip(probs, dprob, parts)
        ]
        gv = [dot(x.astype(BF), b, NN) for x, b in zip(probs, grad)]
        gk = [dot(x, b, NN) for x, b in zip(dscore, quer)]
        gq = [dot(x, b, TN) for x, b in zip(dscore, keys)]
        for p, a, b, c in zip(parts, gv, gk, gq):
            at = p[4] * NCHIP + p[5]
            dkv[at, BLK:] += a
            dkv[at, :BLK] += b
            dq[p[0] * QPER + p[1]] += c
        return carry

    lax.fori_loop(0, steps, body, 0)
    sends = []
    for r, ref in enumerate((dq0, dq1, dq2, dq3)):
        part = slice(r * QPER, (r + 1) * QPER)
        dqs[part] = dq[part].astype(BF)
        sends.append(pltpu.make_async_copy(dqs.at[part], ref, outsems.at[r]))
        sends[-1].start()
    other[...] = dkv[NCHIP:].astype(BF)
    own[...] = dkv[:NCHIP].astype(BF)
    for send in sends:
        send.wait()


def backward(ents, stats, xparts, kvs):
    smem = pl.BlockSpec(memory_space=pltpu.SMEM)
    vmem = pl.BlockSpec(memory_space=pltpu.VMEM)
    far = pl.BlockSpec(memory_space=pl.ANY)
    tile = (BLK, DH)
    outs = [jax.ShapeDtypeStruct((QPER,) + tile, BF)] * 4
    pair = (NCHIP, 2 * BLK, DH)
    outs += [jax.ShapeDtypeStruct(pair, BF)] * 2
    return pl.pallas_call(
        bwd_kernel,
        out_shape=tuple(outs),
        in_specs=[smem] + [vmem] * 4 + [far] * 10,
        out_specs=tuple([far] * 4 + [vmem] * 2),
        scratch_shapes=scratch_in()
        + [
            pltpu.VMEM((NQ,) + tile, F32),
            pltpu.VMEM((NB, 2 * BLK, DH), F32),
            pltpu.VMEM((NQ,) + tile, BF),
            pltpu.VMEM((2 * NQ, DH), F32),
            pltpu.VMEM((2 * NQ, DH), F32),
            pltpu.SemaphoreType.DMA((NCOPY,)),
            pltpu.SemaphoreType.DMA((NZ,)),
        ],
        compiler_params=pltpu.CompilerParams(vmem_limit_bytes=24 * MB),
        name="backward",
    )(ents, *stats, *xparts, *kvs)


def place_parts(z, parts, sems):
    copies = []
    for n, (r, ref, out) in enumerate(parts):
        rows = pl.ds(pl.multiple_of(((z + r) & 3) * BLK, BLK), BLK)
        copies.append(pltpu.make_async_copy(ref, out.at[rows], sems.at[n]))
    for copy in copies:
        copy.start()
    for copy in copies:
        copy.wait()


def near_kernel(k0, k1, k3, v0, v1, v3, outk, outv, sems):
    parts = [(0, k0, outk), (1, k1, outk), (3, k3, outk)]
    parts += [(0, v0, outv), (1, v1, outv), (3, v3, outv)]
    place_parts(position()[0], parts, sems)


def far_kernel(k2, v2, ink, inv, outk, outv, held, insems, outsems):
    z = position()[0]
    rows = BLK // CHUNKS
    came, went = [], []
    for n in range(CHUNKS):
        for t, (ref, out) in enumerate(((k2, outk), (v2, outv))):
            at = pl.ds(n * rows, rows)
            to = pl.ds(pl.multiple_of(((z + 2) & 3) * BLK + n * rows, rows), rows)
            s = 2 * n + t
            came.append(pltpu.make_async_copy(ref.at[at], held.at[t, at], insems.at[s]))
            went.append(pltpu.make_async_copy(held.at[t, at], out.at[to], outsems.at[s]))
    for copy in came:
        copy.start()
    for first, second in zip(came, went):
        first.wait()
        second.start()
    for copy in went:
        copy.wait()


def place_near(kparts, vparts):
    smem = pl.BlockSpec(memory_space=pltpu.SMEM)
    vmem = pl.BlockSpec(memory_space=pltpu.VMEM)
    far = pl.BlockSpec(memory_space=pl.ANY)
    shape = jax.ShapeDtypeStruct((NZ * BLK, H * DH), BF)
    return pl.pallas_call(
        near_kernel,
        out_shape=(shape, shape),
        in_specs=[vmem] * 6,
        out_specs=(far, far),
        scratch_shapes=[pltpu.SemaphoreType.DMA((6,))],
        compiler_params=pltpu.CompilerParams(vmem_limit_bytes=8 * MB),
        name="place_near",
    )(*kparts, *vparts)


def place_far(near, k_far, v_far):
    far = pl.BlockSpec(memory_space=pl.ANY)
    shape = jax.ShapeDtypeStruct((NZ * BLK, H * DH), BF)
    return pl.pallas_call(
        far_kernel,
        out_shape=(shape, shape),
        in_specs=[far] * 4,
        out_specs=(far, far),
        scratch_shapes=[
            pltpu.VMEM((2, BLK, H * DH), BF),
            pltpu.SemaphoreType.DMA((2 * CHUNKS,)),
            pltpu.SemaphoreType.DMA((2 * CHUNKS,)),
        ],
        input_output_aliases={2: 0, 3: 1},
        compiler_params=pltpu.CompilerParams(vmem_limit_bytes=8 * MB),
        name="place_far",
    )(k_far, v_far, *near)


def heads_first(array):
    return jnp.transpose(array.reshape(array.shape[0], H, DH), (1, 0, 2))


def rows_first(array):
    return jnp.transpose(array, (1, 0, 2)).reshape(array.shape[1], H * DH)


def per_device(queries, grad_out, mem_keys, mem_values, block_lists, block_home):
    k = lax.axis_index("mem") & 1
    q_own, g_own, kv_cat = prepare(queries, grad_out, mem_keys, mem_values)
    lists = tuple(over_z(block_lists, shift) for shift in (-1, 2, 1))
    kv_cat, lists = lax.optimization_barrier((kv_cat, lists))
    ents = make_list((block_lists,) + lists, block_home)
    q_prev = over_z(q_own, 1)
    g_next = over_z(g_own, -1)
    g_prev = over_z(g_own, 1)
    q_next = over_z(q_own, -1)
    kv_own, q_prev, g_next, g_prev, q_next, ents = lax.optimization_barrier(
        (plane_exchange(kv_cat), q_prev, g_next, g_prev, q_next, ents)
    )
    q_far = over_z(q_prev, 1)
    g_far = over_z(g_next, -1)
    kvs = (kv_own, swap_cores(kv_own))
    xparts = (q_own, q_next, q_far, q_prev, g_own, g_next, g_far, g_prev)

    stat = jnp.zeros((3, NQ, DH), F32)
    stat = forward(EARLY, 0, ents, stat, (q_own, q_next, q_prev), (g_own, g_next, g_prev), kvs)
    stat = forward(LATE, LATE_AT, ents, stat, (q_far,), (g_far,), kvs)
    stats = (stat, over_z(stat, 1), over_z(stat, 2), over_z(stat, -1))
    dq0, dq1, dq2, dq3, own, other = backward(ents, stats, xparts, kvs)

    both = (own.astype(F32) + swap_cores(other).astype(F32)).astype(BF)
    got = plane_exchange(both)
    k_own, v_own = rows_first(got[:, :BLK]), rows_first(got[:, BLK:])
    v_prev = over_z(v_own, 1)
    v_next = over_z(v_own, -1)
    k_next = over_z(k_own, -1)
    k_prev = over_z(k_own, 1)
    dq_sum = (
        dq0.astype(F32)
        + over_z(dq1, 1).astype(F32)
        + over_z(dq3, -1).astype(F32)
        + over_z(dq2, 2).astype(F32)
    ).astype(BF)
    half = BLK // 2
    keep = lax.dynamic_slice_in_dim(dq_sum, k * half, half, 1)
    give = lax.dynamic_slice_in_dim(dq_sum, (1 - k) * half, half, 1)
    got = swap_cores(give)
    whole = jnp.where(
        k == 0, jnp.concatenate([keep, got], axis=0), jnp.concatenate([got, keep], axis=0)
    )
    whole, v_prev, k_next = lax.optimization_barrier((whole, v_prev, k_next))
    v_far = over_z(v_prev, 1)
    k_far = over_z(k_next, -1)
    near = place_near((k_own, k_next, k_prev), (v_own, v_next, v_prev))
    grad_keys, grad_values = place_far(near, k_far, v_far)
    grad_queries = rows_first(plane_exchange(whole))
    return grad_queries, grad_keys, grad_values


def solution(mesh):
    in_specs = (P("dp", None), P("dp", None), P("mem", None), P("mem", None), P("dp", None), P())
    out_specs = (P(("dp", "mem"), None), P("mem", None), P("mem", None))
    return jax.shard_map(
        per_device, mesh=mesh, in_specs=in_specs, out_specs=out_specs, check_vma=False
    )
```

```python
import functools

import jax
import jax.numpy as jnp
from jax import lax
from jax.experimental import pallas as pl
from jax.experimental.pallas import tpu as pltpu
from jax.sharding import PartitionSpec as P

H = 16
DH = 128
BLK = 128
TOPB = 16
NZ = 4
NCHIP = 16
QPER = 8
NQ = NZ * QPER
NB = 2 * NCHIP
NENT = NQ * TOPB
EARLY = (0, 1, 3)
LATE = (2,)
LATE_AT = len(EARLY) * QPER * TOPB + 8
COUNT = LATE_AT + len(LATE) * QPER * TOPB + 16
NCOPY = 2 * NZ + 2
UNROLL_F = 8
UNROLL_B = 16
SCALE = DH ** (-0.5)
BF = jnp.bfloat16
F32 = jnp.float32
MB = 1 << 20


NT = (((1,), (1,)), ((), ()))
NN = (((1,), (0,)), ((), ()))
TN = (((0,), (0,)), ((), ()))


def position():
    m = lax.axis_index("mem")
    return lax.axis_index("dp"), m >> 1, m & 1


def dot(a, b, dims):
    return lax.dot_general(a, b, dims, preferred_element_type=F32)


def over_z(array, shift):
    return lax.ppermute(array, "dp", [(i, (i + shift) % NZ) for i in range(NZ)])


def swap_cores(array):
    return lax.ppermute(array, "mem", [(i, i ^ 1) for i in range(2 * NCHIP)])


def plane_exchange(array):
    groups = [[2 * c + k for c in range(NCHIP)] for k in range(2)]
    return lax.all_to_all(array, "mem", 0, 0, axis_index_groups=groups)


def prepare_kernel(queries, grads, keys, values, q, g, kv, sems):
    z, c, k = position()
    cols = pl.ds(pl.multiple_of(c * DH, DH), DH)
    pairs = []
    for i in range(QPER):
        rows = pl.ds(pl.multiple_of((k * QPER + i) * BLK, BLK), BLK)
        pairs.append((queries.at[rows, cols], q.at[i]))
        pairs.append((grads.at[rows, cols], g.at[i]))
    rows = pl.ds(pl.multiple_of(z * BLK, BLK), BLK)
    for h in range(H):
        cols = slice(h * DH, (h + 1) * DH)
        pairs.append((keys.at[rows, cols], kv.at[h, :BLK]))
        pairs.append((values.at[rows, cols], kv.at[h, BLK:]))
    copies = [pltpu.make_async_copy(a, b, sems.at[n]) for n, (a, b) in enumerate(pairs)]
    for copy in copies:
        copy.start()
    for copy in copies:
        copy.wait()


def prepare(queries, grads, keys, values):
    vmem = pl.BlockSpec(memory_space=pltpu.VMEM)
    far = pl.BlockSpec(memory_space=pl.ANY)
    return pl.pallas_call(
        prepare_kernel,
        out_shape=(
            jax.ShapeDtypeStruct((QPER, BLK, DH), BF),
            jax.ShapeDtypeStruct((QPER, BLK, DH), BF),
            jax.ShapeDtypeStruct((H, 2 * BLK, DH), BF),
        ),
        in_specs=[far] * 4,
        out_specs=(vmem, vmem, vmem),
        scratch_shapes=[pltpu.SemaphoreType.DMA((2 * QPER + 2 * H,))],
        compiler_params=pltpu.CompilerParams(vmem_limit_bytes=60 * MB),
        name="prepare",
    )(queries, grads, keys, values)


def list_kernel(l0, l1, l2, l3, home, ents):
    z, _, k = position()

    def group(r, lists, n):
        def block(i, n):
            q = r * QPER + i
            seen = jnp.int32(0)
            for t in range(TOPB):
                slot = home[lists[k * QPER + i, t]]
                mine = (slot & 3) == z
                owner = slot >> 2
                b = ((owner & 1) ^ k) * NCHIP + (owner >> 1)
                ents[n] = (q << 15) | ((seen * NQ + q) << 5) | b
                step = mine.astype(jnp.int32)
                n = n + step
                seen = seen + step
            return n

        return lax.fori_loop(0, QPER, block, n)

    every = (l0, l1, l2, l3)
    for part, (start, groups) in enumerate(((0, EARLY), (LATE_AT, LATE))):
        n = jnp.int32(start)
        for r in groups:
            n = group(r, every[r], n)
        for u in range(8 if start == 0 else 16):
            ents[n + u] = ((NQ + groups[0] * QPER) << 15) | (NENT << 5)
        ents[COUNT + part] = n - start


def make_list(lists, home):
    smem = pl.BlockSpec(memory_space=pltpu.SMEM)
    return pl.pallas_call(
        list_kernel,
        out_shape=jax.ShapeDtypeStruct((COUNT + 8,), jnp.int32),
        in_specs=[smem] * 5,
        out_specs=smem,
        compiler_params=pltpu.CompilerParams(vmem_limit_bytes=MB),
        name="entry_list",
    )(*lists, home)


def fetch(groups, qrefs, grefs, kvrefs, qs, gs, kv, sems):
    pairs = [(ref, kv.at[p]) for p, ref in enumerate(kvrefs)]
    pairs += [(ref, qs.at[r]) for r, ref in zip(groups, qrefs)]
    pairs += [(ref, gs.at[r]) for r, ref in zip(groups, grefs)]
    copies = [pltpu.make_async_copy(a, b, sems.at[n]) for n, (a, b) in enumerate(pairs)]
    for copy in copies:
        copy.start()
    return copies


def unpack(p):
    q = p >> 15
    b = p & 31
    return (q >> 3) & 3, q & 7, q, (p >> 5) & 1023, b >> 4, b & 15


def fwd_kernel(groups, start, ents, before, *refs):
    size = len(groups)
    out, qs, gs, kv, st, sems = refs[2 * size + 2 :]
    copies = fetch(
        groups, refs[:size], refs[size : 2 * size], refs[2 * size : 2 * size + 2], qs, gs, kv, sems
    )
    st[0] = jnp.full((NENT + 8, DH), -1e30, F32)
    st[1] = jnp.zeros((NENT + 8, DH), F32)
    st[2] = jnp.zeros((NENT + 8, DH), F32)
    for copy in copies:
        copy.wait()

    def body(n, carry):
        parts = [unpack(ents[start + UNROLL_F * n + u]) for u in range(UNROLL_F)]
        scores = [dot(kv[p[4], p[5], :BLK], qs[p[0], p[1]], NT) * SCALE for p in parts]
        dprob = [dot(kv[p[4], p[5], BLK:], gs[p[0], p[1]], NT) for p in parts]
        highs = [jnp.max(x, axis=0, keepdims=True) for x in scores]
        expo = [jnp.exp(x - high) for x, high in zip(scores, highs)]
        for p, high, e, d in zip(parts, highs, expo, dprob):
            row = pl.ds(p[3], 1)
            st[0, row, :] = high
            st[1, row, :] = jnp.sum(e, axis=0, keepdims=True)
            st[2, row, :] = jnp.sum(e.astype(BF).astype(F32) * d, axis=0, keepdims=True)
        return carry

    part = 0 if start == 0 else 1
    lax.fori_loop(0, (ents[COUNT + part] + UNROLL_F - 1) // UNROLL_F, body, 0)
    out[...] = before[...]
    for r in groups:
        rows = [slice(e * NQ + r * QPER, e * NQ + (r + 1) * QPER) for e in range(TOPB)]
        high = st[0, rows[0]]
        for row in rows[1:]:
            high = jnp.maximum(high, st[0, row])
        total = jnp.zeros((QPER, DH), F32)
        prod = jnp.zeros((QPER, DH), F32)
        for row in rows:
            weight = jnp.exp(st[0, row] - high)
            total = total + weight * st[1, row]
            prod = prod + weight * st[2, row]
        at = slice(r * QPER, (r + 1) * QPER)
        out[0, at] = high
        out[1, at] = total
        out[2, at] = prod


def scratch_in():
    return [
        pltpu.VMEM((NZ, QPER, BLK, DH), BF),
        pltpu.VMEM((NZ, QPER, BLK, DH), BF),
        pltpu.VMEM((2, NCHIP, 2 * BLK, DH), BF),
    ]


def forward(groups, start, ents, before, qparts, gparts, kvs):
    smem = pl.BlockSpec(memory_space=pltpu.SMEM)
    vmem = pl.BlockSpec(memory_space=pltpu.VMEM)
    far = pl.BlockSpec(memory_space=pl.ANY)
    return pl.pallas_call(
        functools.partial(fwd_kernel, groups, start),
        out_shape=jax.ShapeDtypeStruct((3, NQ, DH), F32),
        in_specs=[smem, vmem] + [far] * (2 * len(groups) + 2),
        out_specs=vmem,
        scratch_shapes=scratch_in()
        + [pltpu.VMEM((3, NENT + 8, DH), F32), pltpu.SemaphoreType.DMA((NCOPY,))],
        compiler_params=pltpu.CompilerParams(vmem_limit_bytes=14 * MB),
        name="forward",
    )(ents, before, *qparts, *gparts, *kvs)


def bwd_kernel(
    ents, s0, s1, s2, s3, q0, q1, q2, q3, g0, g1, g2, g3, kva, kvb,
    dq0, dq1, dq2, dq3, own, other,
    qs, gs, kv, dq, dkv, dqs, lse, delta, sems, outsems,
):
    copies = fetch(range(NZ), (q0, q1, q2, q3), (g0, g1, g2, g3), (kva, kvb), qs, gs, kv, sems)

    def clear(i, carry):
        zero = jnp.zeros((BLK, DH), F32)
        dq[i] = zero
        dkv[i, :BLK] = zero
        dkv[i, BLK:] = zero
        return carry

    lax.fori_loop(0, NQ, clear, 0)
    for r in range(NZ):
        rows = slice(r * QPER, (r + 1) * QPER)
        parts = []
        for ref, shift in ((s0, 0), (s1, 1), (s2, 2), (s3, 3)):
            at = (r + shift) % NZ
            parts.append([ref[n, at * QPER : (at + 1) * QPER] for n in range(3)])
        high = jnp.maximum(
            jnp.maximum(parts[0][0], parts[1][0]), jnp.maximum(parts[2][0], parts[3][0])
        )
        total = jnp.zeros((QPER, DH), F32)
        prod = jnp.zeros((QPER, DH), F32)
        for part in parts:
            weight = jnp.exp(part[0] - high)
            total = total + weight * part[1]
            prod = prod + weight * part[2]
        lse[rows] = high + jnp.log(total)
        delta[rows] = prod / total
    for copy in copies:
        copy.wait()

    lse[NQ:] = jnp.full((NQ, DH), 1e30, F32)
    delta[NQ:] = jnp.zeros((NQ, DH), F32)

    early = ents[COUNT]
    steps = (early + ents[COUNT + 1] + UNROLL_B - 1) // UNROLL_B

    def body(n, carry):
        parts = []
        for u in range(UNROLL_B):
            at = n * UNROLL_B + u
            parts.append(unpack(ents[jnp.where(at < early, at, at + (LATE_AT - early))]))
        keys = [kv[p[4], p[5], :BLK] for p in parts]
        quer = [qs[p[0], p[1]] for p in parts]
        grad = [gs[p[0], p[1]] for p in parts]
        scores = [dot(a, b, NT) * SCALE for a, b in zip(keys, quer)]
        dprob = [dot(kv[p[4], p[5], BLK:], b, NT) for p, b in zip(parts, grad)]
        probs = [jnp.exp(x - lse[pl.ds(p[2], 1), :]) for x, p in zip(scores, parts)]
        dscore = [
            (x * (d - delta[pl.ds(p[2], 1), :]) * SCALE).astype(BF)
            for x, d, p in zip(probs, dprob, parts)
        ]
        probs = [x.astype(BF) for x in probs]
        for p, x, d, key, que, gra in zip(parts, probs, dscore, keys, quer, grad):
            at = p[4] * NCHIP + p[5]
            dkv[at, BLK:] += dot(x, gra, NN)
            dkv[at, :BLK] += dot(d, que, NN)
            dq[p[0] * QPER + p[1]] += dot(d, key, TN)
        return carry

    lax.fori_loop(0, steps, body, 0)
    sends = []
    for r, ref in enumerate((dq0, dq1, dq2, dq3)):
        part = slice(r * QPER, (r + 1) * QPER)
        dqs[part] = dq[part].astype(BF)
        sends.append(pltpu.make_async_copy(dqs.at[part], ref, outsems.at[r]))
        sends[-1].start()
    other[...] = dkv[NCHIP:].astype(BF)
    own[...] = dkv[:NCHIP].astype(BF)
    for send in sends:
        send.wait()


def backward(ents, stats, xparts, kvs):
    smem = pl.BlockSpec(memory_space=pltpu.SMEM)
    vmem = pl.BlockSpec(memory_space=pltpu.VMEM)
    far = pl.BlockSpec(memory_space=pl.ANY)
    tile = (BLK, DH)
    outs = [jax.ShapeDtypeStruct((QPER,) + tile, BF)] * 4
    pair = (NCHIP, 2 * BLK, DH)
    outs += [jax.ShapeDtypeStruct(pair, BF)] * 2
    return pl.pallas_call(
        bwd_kernel,
        out_shape=tuple(outs),
        in_specs=[smem] + [vmem] * 4 + [far] * 10,
        out_specs=tuple([far] * 4 + [vmem] * 2),
        scratch_shapes=scratch_in()
        + [
            pltpu.VMEM((NQ,) + tile, F32),
            pltpu.VMEM((NB, 2 * BLK, DH), F32),
            pltpu.VMEM((NQ,) + tile, BF),
            pltpu.VMEM((2 * NQ, DH), F32),
            pltpu.VMEM((2 * NQ, DH), F32),
            pltpu.SemaphoreType.DMA((NCOPY,)),
            pltpu.SemaphoreType.DMA((NZ,)),
        ],
        compiler_params=pltpu.CompilerParams(vmem_limit_bytes=24 * MB),
        name="backward",
    )(ents, *stats, *xparts, *kvs)


def place_parts(z, parts, sems):
    copies = []
    for n, (r, ref, out) in enumerate(parts):
        rows = pl.ds(pl.multiple_of(((z + r) & 3) * BLK, BLK), BLK)
        copies.append(pltpu.make_async_copy(ref, out.at[rows], sems.at[n]))
    for copy in copies:
        copy.start()
    for copy in copies:
        copy.wait()


def near_kernel(k0, k1, k3, v0, v1, v3, outk, outv, sems):
    parts = [(0, k0, outk), (1, k1, outk), (3, k3, outk)]
    parts += [(0, v0, outv), (1, v1, outv), (3, v3, outv)]
    place_parts(position()[0], parts, sems)


def far_kernel(k2, v2, ink, inv, outk, outv, sems):
    place_parts(position()[0], [(2, k2, outk), (2, v2, outv)], sems)


def place_near(kparts, vparts):
    smem = pl.BlockSpec(memory_space=pltpu.SMEM)
    vmem = pl.BlockSpec(memory_space=pltpu.VMEM)
    far = pl.BlockSpec(memory_space=pl.ANY)
    shape = jax.ShapeDtypeStruct((NZ * BLK, H * DH), BF)
    return pl.pallas_call(
        near_kernel,
        out_shape=(shape, shape),
        in_specs=[vmem] * 6,
        out_specs=(far, far),
        scratch_shapes=[pltpu.SemaphoreType.DMA((6,))],
        compiler_params=pltpu.CompilerParams(vmem_limit_bytes=8 * MB),
        name="place_near",
    )(*kparts, *vparts)


def place_far(near, k_far, v_far):
    far = pl.BlockSpec(memory_space=pl.ANY)
    shape = jax.ShapeDtypeStruct((NZ * BLK, H * DH), BF)
    return pl.pallas_call(
        far_kernel,
        out_shape=(shape, shape),
        in_specs=[pl.BlockSpec(memory_space=pltpu.VMEM)] * 2 + [far] * 2,
        out_specs=(far, far),
        scratch_shapes=[pltpu.SemaphoreType.DMA((2,))],
        input_output_aliases={2: 0, 3: 1},
        compiler_params=pltpu.CompilerParams(vmem_limit_bytes=8 * MB),
        name="place_far",
    )(k_far, v_far, *near)


def heads_first(array):
    return jnp.transpose(array.reshape(array.shape[0], H, DH), (1, 0, 2))


def rows_first(array):
    return jnp.transpose(array, (1, 0, 2)).reshape(array.shape[1], H * DH)


def per_device(queries, grad_out, mem_keys, mem_values, block_lists, block_home):
    k = lax.axis_index("mem") & 1
    q_own, g_own, kv_cat = prepare(queries, grad_out, mem_keys, mem_values)
    lists = tuple(over_z(block_lists, shift) for shift in (-1, 2, 1))
    kv_cat, lists = lax.optimization_barrier((kv_cat, lists))
    ents = make_list((block_lists,) + lists, block_home)
    q_prev = over_z(q_own, 1)
    g_next = over_z(g_own, -1)
    g_prev = over_z(g_own, 1)
    q_next = over_z(q_own, -1)
    kv_own, q_prev, g_next, g_prev, q_next, ents = lax.optimization_barrier(
        (plane_exchange(kv_cat), q_prev, g_next, g_prev, q_next, ents)
    )
    q_far = over_z(q_prev, 1)
    g_far = over_z(g_next, -1)
    kvs = (kv_own, swap_cores(kv_own))
    xparts = (q_own, q_next, q_far, q_prev, g_own, g_next, g_far, g_prev)

    stat = jnp.zeros((3, NQ, DH), F32)
    stat = forward(EARLY, 0, ents, stat, (q_own, q_next, q_prev), (g_own, g_next, g_prev), kvs)
    stat = forward(LATE, LATE_AT, ents, stat, (q_far,), (g_far,), kvs)
    stats = (stat, over_z(stat, 1), over_z(stat, 2), over_z(stat, -1))
    dq0, dq1, dq2, dq3, own, other = backward(ents, stats, xparts, kvs)

    both = (own.astype(F32) + swap_cores(other).astype(F32)).astype(BF)
    got = plane_exchange(both)
    k_own, v_own = rows_first(got[:, :BLK]), rows_first(got[:, BLK:])
    v_prev = over_z(v_own, 1)
    v_next = over_z(v_own, -1)
    k_next = over_z(k_own, -1)
    k_prev = over_z(k_own, 1)
    dq_sum = (
        dq0.astype(F32)
        + over_z(dq1, 1).astype(F32)
        + over_z(dq3, -1).astype(F32)
        + over_z(dq2, 2).astype(F32)
    ).astype(BF)
    half = BLK // 2
    keep = lax.dynamic_slice_in_dim(dq_sum, k * half, half, 1)
    give = lax.dynamic_slice_in_dim(dq_sum, (1 - k) * half, half, 1)
    got = swap_cores(give)
    whole = jnp.where(
        k == 0, jnp.concatenate([keep, got], axis=0), jnp.concatenate([got, keep], axis=0)
    )
    whole, v_prev, k_next = lax.optimization_barrier((whole, v_prev, k_next))
    v_far = over_z(v_prev, 1)
    k_far = over_z(k_next, -1)
    near = place_near((k_own, k_next, k_prev), (v_own, v_next, v_prev))
    grad_keys, grad_values = place_far(near, k_far, v_far)
    grad_queries = rows_first(plane_exchange(whole))
    return grad_queries, grad_keys, grad_values


def solution(mesh):
    in_specs = (P("dp", None), P("dp", None), P("mem", None), P("mem", None), P("dp", None), P())
    out_specs = (P(("dp", "mem"), None), P("mem", None), P("mem", None))
    return jax.shard_map(
        per_device, mesh=mesh, in_specs=in_specs, out_specs=out_specs, check_vma=False
    )
```
